32 devices in a mesh: dp: 8 (over z, core), seq: 4 (over y, x).
Axes of the slice: x: 2, y: 2, z: 4, core: 2. Of those that a mesh axis runs over, the one named last changes fastest.
Arguments:
- hidden_in: bfloat16 [8, 512, 2048], P('dp', 'seq'), may hold values from -6 to 6
- boundary: int32 [8, 4], P('dp'), may hold values from 1 to 511, as said below
- norm_gain: float32 [2048], replicated, may hold values from 0.5 to 1.5
- proj_weight: bfloat16 [2048, 12288], P(('dp', 'seq')), may hold values from -0.125 to 0.125
- rate_weight: bfloat16 [2048, 32], P(('dp', 'seq')), may hold values from -0.125 to 0.125
- conv_weight: float32 [4, 8192], replicated, may hold values from -3 to 3
- log_rate: float32 [16], replicated, may hold values from -8 to 0
- rate_bias: float32 [16], replicated, may hold values from -4 to 4
- head_gain: float32 [256], replicated, may hold values from 0.5 to 1.5
- out_weight: bfloat16 [2048, 4096], P(('dp', 'seq')), may hold values from -0.09375 to 0.09375
- ffn_norm_gain: float32 [2048], replicated, may hold values from 0.5 to 1.5
- gate_up_weight: bfloat16 [2048, 11008], P(('dp', 'seq')), may hold values from -0.125 to 0.125
- down_weight: bfloat16 [2048, 5504], P(('dp', 'seq')), may hold values from -0.078125 to 0.078125
- grad_out: bfloat16 [8, 512, 2048], P('dp', 'seq'), may hold values from -6 to 6
Outputs:
- result: bfloat16 [8, 512, 2048], P('dp', 'seq')
- grad_in: bfloat16 [8, 512, 2048], P('dp', 'seq')
- final_state: float32 [8, 16, 256, 128], P('dp')
- grad_norm_gain: float32 [2048], replicated
- grad_proj_weight: float32 [2048, 12288], P(('dp', 'seq'))
- grad_rate_weight: float32 [2048, 32], P(('dp', 'seq'))
- grad_conv_weight: float32 [4, 8192], replicated
- grad_log_rate: float32 [16], replicated
- grad_rate_bias: float32 [16], replicated
- grad_head_gain: float32 [256], replicated
- grad_out_weight: float32 [2048, 4096], P(('dp', 'seq'))
- grad_ffn_norm_gain: float32 [2048], replicated
- grad_gate_up_weight: float32 [2048, 11008], P(('dp', 'seq'))
- grad_down_weight: float32 [2048, 5504], P(('dp', 'seq'))
The draws below stay inside these ranges and needn't reach their ends.
Inputs may be any that keep to these rules, and one draw needn't show every extreme that they name: `boundary`: in each row the first entry lies among the first 128 positions and the others among the last 128 positions.
All inputs are finite; a program needn't handle non-finite values.
Results may differ from the reference program's by a relative error of at most 0.019.
The reference program's roundings to bfloat16 on the way count: a program that leaves them out, or rounds other values in their place, can miss the bound.
Values may be sent and summed in bfloat16 or wider, within the bound.
No kernel may reach another device: no remote copies, remote signals or barrier semaphores. Data moves between devices by JAX's collectives and lax.ppermute only.
A program may use at most 608 MiB of HBM per device.

```python
import jax
import jax.numpy as jnp
from jax import lax

D = 2048
HEADS = 16
KEY = 128
VALUE = 256
FF = 5504
CONV = 4
GROUP = 64
BOUNDS = 4
TOK_DEV = 128
ROW = 512
ROWS = 8
HK = 2048
HV = 4096
CHANNELS = 8192


def draw_boundary(key, part):
    key = jax.random.fold_in(key, 11)
    head_key, tail_key = jax.random.split(key)
    first = jax.random.randint(head_key, (ROWS, 1), 1, TOK_DEV)
    others = jax.random.randint(tail_key, (ROWS, BOUNDS - 1), ROW - TOK_DEV, ROW)
    first = first.at[0, 0].set(1)
    others = others.at[0, BOUNDS - 2].set(ROW - 1)
    return jnp.concatenate([first, others], axis=1).astype(jnp.int32)


def levels(rng, dims, cuts, least, top_value):
    loudness = 1.0
    for position, shards_of in cuts:
        heights = jax.random.uniform(jax.random.fold_in(jax.random.fold_in(rng, 6), position), (shards_of,), jnp.float32, least / len(cuts), top_value / len(cuts))
        loudness = loudness * jnp.repeat(jnp.exp(heights), dims[position] // shards_of).reshape((-1,) + (1,) * (len(dims) - 1 - position))
    return loudness


def bell_draw(own_key, shape, spread, limit, shards=(), kind=jnp.bfloat16):
    values = jax.random.normal(own_key, shape, jnp.float32) * spread
    if len(shards) > 0:
        values = levels(own_key, shape, shards, -0.22, 0.18) * values
    return jnp.clip(values, min=-limit, max=limit).astype(kind)


def setup_inputs(seed: int = 0) -> dict:
    keys = jax.random.split(jax.random.key(seed), 15)
    hidden_in = bell_draw(keys[0], (ROWS, ROW, D), 1.0, 6.0, ((0, 8), (1, 4)))
    boundary = draw_boundary(jax.random.fold_in(keys[14], 71), 0)
    norm_gain = jnp.clip(1.0 + 0.1 * jax.random.normal(keys[2], (D,), jnp.float32), 0.5, 1.5)
    proj_weight = bell_draw(keys[3], (D, 2 * HK + 2 * HV), D ** -0.5, 0.125, ((0, 32),))
    rate_weight = bell_draw(keys[4], (D, 2 * HEADS), D ** -0.5, 0.125, ((0, 32),))
    conv_weight = bell_draw(keys[5], (CONV, CHANNELS), 0.5, 3.0, (), jnp.float32)
    log_rate = jnp.clip(jax.random.uniform(keys[6], (HEADS,), jnp.float32, -8.0, 0.0), -8.0, 0.0)
    rate_bias = bell_draw(keys[7], (HEADS,), 1.0, 4.0, (), jnp.float32)
    head_gain = jnp.clip(1.0 + 0.1 * jax.random.normal(keys[8], (VALUE,), jnp.float32), 0.5, 1.5)
    out_weight = bell_draw(keys[9], (D, HV), HV ** -0.5, 0.09375, ((0, 32),))
    ffn_norm_gain = jnp.clip(1.0 + 0.1 * jax.random.normal(keys[10], (D,), jnp.float32), 0.5, 1.5)
    gate_up_weight = bell_draw(keys[11], (D, 2 * FF), D ** -0.5, 0.125, ((0, 32),))
    down_weight = bell_draw(keys[12], (D, FF), FF ** -0.5, 0.078125, ((0, 32),))
    grad_out = bell_draw(keys[13], (ROWS, ROW, D), 1.0, 6.0, ((0, 8), (1, 4)))
    return dict(hidden_in=hidden_in, boundary=boundary, norm_gain=norm_gain, proj_weight=proj_weight, rate_weight=rate_weight, conv_weight=conv_weight, log_rate=log_rate, rate_bias=rate_bias, head_gain=head_gain, out_weight=out_weight, ffn_norm_gain=ffn_norm_gain, gate_up_weight=gate_up_weight, down_weight=down_weight, grad_out=grad_out)


EPS = 1e-06
HIGH = lax.Precision.HIGHEST

@jax.custom_vjp
def low(v):
    return lax.optimization_barrier(v.astype(jnp.bfloat16)).astype(jnp.float32)

@jax.custom_vjp
def low_back(v):
    return v

def low_keep(v):
    return (low(v), None)

def low_pass(kept, grad):
    return (grad,)

def back_keep(v):
    return (v, None)

def back_low(kept, grad):
    return (low(grad),)
low.defvjp(low_keep, low_pass)
low_back.defvjp(back_keep, back_low)

def batched(left, right):
    return jnp.einsum('hij,hjk->hik', left, right, precision=HIGH)

def group_pass(state, block):
    query, key_rows, value_rows, decay_log, beta, start = block
    size = query.shape[0]
    cumulative = jnp.cumsum(decay_log, axis=0)
    segment = jnp.cumsum(start)
    alive = (segment == 0.0).astype(jnp.float32)
    index = jnp.arange(size)
    joined = jnp.logical_and(index[:, None] >= index[None, :], segment[:, None] == segment[None, :])
    strict = (index[:, None] > index[None, :]).astype(jnp.float32)
    joined_f = joined.astype(jnp.float32)
    gap = cumulative.T[:, :, None] - cumulative.T[:, None, :]
    pair = jnp.exp(jnp.where(joined[None], gap, 0.0)) * joined_f[None]
    head_decay = jnp.exp(cumulative) * alive[:, None]
    keys_keys = jnp.einsum('ihk,jhk->hij', key_rows, key_rows, precision=HIGH)
    negated = -(beta.T[:, :, None] * pair * keys_keys * strict[None])
    identity = jnp.broadcast_to(jnp.eye(size, dtype=jnp.float32), negated.shape)
    key_state = jnp.einsum('ihk,hvk->hiv', key_rows, state, precision=HIGH)
    targets = beta.T[:, :, None] * (jnp.transpose(value_rows, (1, 0, 2)) - head_decay.T[:, :, None] * key_state)
    inverse = identity + negated
    power = negated
    for level in range(size.bit_length() - 2):
        power = batched(power, power)
        inverse = batched(inverse, identity + power)
    updates = batched(inverse, targets)
    query_keys = jnp.einsum('ihk,jhk->hij', query, key_rows, precision=HIGH) * pair
    query_state = jnp.einsum('ihk,hvk->hiv', query, state, precision=HIGH)
    output = head_decay.T[:, :, None] * query_state + batched(query_keys, updates)
    last_row = pair[:, size - 1, :]
    carried = jnp.einsum('hj,hjv,jhk->hvk', last_row, updates, key_rows, precision=HIGH)
    new_state = head_decay[size - 1][:, None, None] * state + carried
    return (new_state, jnp.transpose(output, (1, 0, 2)))

def seq_pass(state, query, key_rows, value_rows, decay_log, beta, start, block):
    length = query.shape[0]
    count = length // block
    pieces = tuple((arr.reshape((count, block) + arr.shape[1:]) for arr in (query, key_rows, value_rows, decay_log, beta, start)))
    final, outputs = lax.scan(jax.checkpoint(group_pass), state, pieces)
    return (final, outputs.reshape((length,) + outputs.shape[2:]))

def row_forward(weights, row, bounds):
    norm_gain, proj_weight, rate_weight, conv_weight, log_rate, rate_bias, head_gain, out_weight, ffn_norm_gain, gate_up_weight, down_weight = weights
    length = row.shape[0]
    positions = jnp.arange(length)
    start = jnp.logical_or(jnp.any(positions[:, None] == bounds[None, :], axis=1), positions == 0).astype(jnp.float32)
    scale = lax.rsqrt(lax.optimization_barrier(jnp.mean(row * row, axis=1, keepdims=True)) + EPS)
    first_in = low(row * scale * norm_gain)
    projected = low_back(jnp.dot(first_in, proj_weight, precision=HIGH))
    rates = low_back(jnp.dot(first_in, rate_weight, precision=HIGH))
    channels = 2 * HK + HV
    conv_in = low(projected[:, :channels])
    out_gate = projected[:, channels:]
    padded = jnp.concatenate([jnp.zeros((CONV - 1, channels), jnp.float32), conv_in], axis=0)
    start_pad = jnp.concatenate([jnp.zeros((CONV - 2,), jnp.float32), start], axis=0)
    conv_out = conv_weight[CONV - 1] * conv_in
    keep = jnp.ones((length,), jnp.float32)
    for lag in range(1, CONV):
        keep = keep * (1.0 - start_pad[CONV - 1 - lag:CONV - 1 - lag + length])
        conv_out = conv_out + conv_weight[CONV - 1 - lag] * padded[CONV - 1 - lag:CONV - 1 - lag + length] * keep[:, None]
    act = jax.nn.silu(conv_out)
    query = act[:, :HK].reshape(length, HEADS, KEY)
    key_rows = act[:, HK:2 * HK].reshape(length, HEADS, KEY)
    values = act[:, 2 * HK:].reshape(length, HEADS, VALUE)
    query = query * lax.rsqrt(lax.optimization_barrier(jnp.sum(query * query, axis=2, keepdims=True)) + EPS) * KEY ** (-0.5)
    key_rows = key_rows * lax.rsqrt(lax.optimization_barrier(jnp.sum(key_rows * key_rows, axis=2, keepdims=True)) + EPS)
    query = low(low_back(query))
    key_rows = low(low_back(key_rows))
    values = low(low_back(values))
    decay_log = -jnp.exp(log_rate) * jax.nn.softplus(rates[:, :HEADS] + rate_bias)
    beta = jax.nn.sigmoid(rates[:, HEADS:])
    state = jnp.zeros((HEADS, VALUE, KEY), jnp.float32)
    final, mixed = seq_pass(state, query, key_rows, values, decay_log, beta, start, GROUP)
    head_scale = lax.rsqrt(lax.optimization_barrier(jnp.mean(mixed * mixed, axis=2, keepdims=True)) + EPS)
    gated = mixed * head_scale * head_gain * jax.nn.silu(out_gate.reshape(length, HEADS, VALUE))
    branch = low(gated.reshape(length, HV))
    hidden = row + low_back(jnp.dot(branch, out_weight.T, precision=HIGH))
    scale_two = lax.rsqrt(lax.optimization_barrier(jnp.mean(hidden * hidden, axis=1, keepdims=True)) + EPS)
    second_in = low(hidden * scale_two * ffn_norm_gain)
    both = low_back(jnp.dot(second_in, gate_up_weight, precision=HIGH))
    inner = low(jax.nn.silu(both[:, :FF]) * both[:, FF:])
    result = hidden + low_back(jnp.dot(inner, down_weight.T, precision=HIGH))
    return (result, final)

def reference(hidden_in, boundary, norm_gain, proj_weight, rate_weight, conv_weight, log_rate, rate_bias, head_gain, out_weight, ffn_norm_gain, gate_up_weight, down_weight, grad_out):
    weights = tuple((arr.astype(jnp.float32) for arr in (norm_gain, proj_weight, rate_weight, conv_weight, log_rate, rate_bias, head_gain, out_weight, ffn_norm_gain, gate_up_weight, down_weight)))
    rows = hidden_in.astype(jnp.float32)

    def forward(params, inputs):

        def one_row(pair):
            return row_forward(params, pair[0], pair[1])
        return lax.map(jax.checkpoint(one_row), (inputs, boundary))
    (result, finals), pullback = jax.vjp(forward, weights, rows)
    grads, row_grads = pullback((grad_out.astype(jnp.float32), jnp.zeros_like(finals)))
    return (result.astype(jnp.bfloat16), row_grads.astype(jnp.bfloat16), finals, grads[0], grads[1], grads[2], grads[3], grads[4], grads[5], grads[6], grads[7], grads[8], grads[9], grads[10])
```

```python
import jax
import jax.numpy as jnp
from jax import lax
from jax.sharding import Mesh
from jax.sharding import PartitionSpec as P

HEADS = 16
KEY = 128
VALUE = 256
FF = 5504
CONV = 4
GROUP = 64
HK = 2048
HV = 4096


EPS = 1e-06
HIGH = lax.Precision.HIGHEST
PLANE = ("core", "seq")


def batched(left, right):
    return jnp.einsum("hij,hjk->hik", left, right, precision=HIGH)


def group_pass(state, block):
    query, key_rows, value_rows, decay_log, beta, start = block
    size = query.shape[0]
    cumulative = jnp.cumsum(decay_log, axis=0)
    segment = jnp.cumsum(start)
    alive = (segment == 0.0).astype(jnp.float32)
    index = jnp.arange(size)
    joined = jnp.logical_and(index[:, None] >= index[None, :], segment[:, None] == segment[None, :])
    strict = (index[:, None] > index[None, :]).astype(jnp.float32)
    joined_f = joined.astype(jnp.float32)
    gap = cumulative.T[:, :, None] - cumulative.T[:, None, :]
    pair = jnp.exp(jnp.where(joined[None], gap, 0.0)) * joined_f[None]
    head_decay = jnp.exp(cumulative) * alive[:, None]
    keys_keys = jnp.einsum("ihk,jhk->hij", key_rows, key_rows, precision=HIGH)
    negated = -(beta.T[:, :, None] * pair * keys_keys * strict[None])
    identity = jnp.broadcast_to(jnp.eye(size, dtype=jnp.float32), negated.shape)
    key_state = jnp.einsum("ihk,hvk->hiv", key_rows, state, precision=HIGH)
    targets = beta.T[:, :, None] * (
        jnp.transpose(value_rows, (1, 0, 2)) - head_decay.T[:, :, None] * key_state
    )
    inverse = identity + negated
    power = negated
    for level in range(size.bit_length() - 2):
        power = batched(power, power)
        inverse = batched(inverse, identity + power)
    updates = batched(inverse, targets)
    query_keys = jnp.einsum("ihk,jhk->hij", query, key_rows, precision=HIGH) * pair
    query_state = jnp.einsum("ihk,hvk->hiv", query, state, precision=HIGH)
    output = head_decay.T[:, :, None] * query_state + batched(query_keys, updates)
    last_row = pair[:, size - 1, :]
    carried = jnp.einsum("hj,hjv,jhk->hvk", last_row, updates, key_rows, precision=HIGH)
    new_state = head_decay[size - 1][:, None, None] * state + carried
    return (new_state, jnp.transpose(output, (1, 0, 2)))


def seq_pass(state, query, key_rows, value_rows, decay_log, beta, start, block):
    length = query.shape[0]
    count = length // block
    pieces = tuple(
        (
            arr.reshape((count, block) + arr.shape[1:])
            for arr in (query, key_rows, value_rows, decay_log, beta, start)
        )
    )
    final, outputs = lax.scan(jax.checkpoint(group_pass), state, pieces)
    return (final, outputs.reshape((length,) + outputs.shape[2:]))


def rounded(value):
    return lax.optimization_barrier(value.astype(jnp.bfloat16)).astype(jnp.float32)


def contract_rows(left, right):
    return lax.dot_general(
        left, right, (((1,), (1,)), ((), ())), preferred_element_type=jnp.float32
    )


def contract_tokens(left, right):
    return lax.dot_general(
        left, right, (((0,), (0,)), ((), ())), preferred_element_type=jnp.float32
    )


def silu_slope(value):
    logistic = jax.nn.sigmoid(value)
    return logistic * (1.0 + value * (1.0 - logistic))


def norm_back(normed, factor, grad):
    return factor * (grad - normed * jnp.mean(grad * normed, axis=-1, keepdims=True))


def unit_back(normed, factor, grad):
    return factor * (grad - normed * jnp.sum(grad * normed, axis=-1, keepdims=True))


def swap_core(x):
    return lax.ppermute(x, "core", [(0, 1), (1, 0)])


def from_peer(x, distance):
    size = lax.axis_size("seq")
    return lax.ppermute(x, "seq", [(i, i ^ distance) for i in range(size)])


def plane_gather(x):
    size, me, core = lax.axis_size("seq"), lax.axis_index("seq"), lax.axis_index("core")
    tokens = x.shape[0]
    row = jnp.zeros((size * tokens, x.shape[1]), x.dtype)
    row = lax.dynamic_update_slice(row, x, (me * tokens, 0))
    for k in range(1, size):
        row = lax.dynamic_update_slice(row, from_peer(x, k), ((me ^ k) * tokens, 0))
    other = swap_core(row)
    first = jnp.where(core == 0, row, other)
    second = jnp.where(core == 0, other, row)
    return jnp.concatenate([first, second], axis=0)


def plane_sum(x):
    size, me, core = lax.axis_size("seq"), lax.axis_index("seq"), lax.axis_index("core")
    half = x.shape[0] // 2
    tokens = half // size
    sent = lax.dynamic_slice_in_dim(x, (1 - core) * half, half, 0).astype(jnp.bfloat16)
    mine = lax.dynamic_slice_in_dim(x, core * half, half, 0)
    row = mine + swap_core(sent).astype(jnp.float32)
    total = lax.dynamic_slice_in_dim(row, me * tokens, tokens, 0)
    for k in range(1, size):
        block = lax.dynamic_slice_in_dim(row, (me ^ k) * tokens, tokens, 0)
        total = total + from_peer(block.astype(jnp.bfloat16), k).astype(jnp.float32)
    return total


def weight_columns(parts, split):
    rows = parts[0].shape[0]
    blocks = [jnp.swapaxes(p.reshape(rows, split, -1), 0, 1) for p in parts]
    blocks = jnp.concatenate(blocks, axis=2) if len(blocks) > 1 else blocks[0]
    blocks = lax.all_to_all(blocks, PLANE, 0, 0)
    return lax.all_gather(blocks.reshape(split * rows, -1), "z", axis=0, tiled=True)


def weight_rows(partial, split):
    mine = lax.psum_scatter(
        partial.astype(jnp.bfloat16), "z", scatter_dimension=0, tiled=True
    )
    blocks = lax.all_to_all(mine.reshape(split, -1, mine.shape[1]), PLANE, 0, 0)
    return jnp.swapaxes(blocks, 0, 1).astype(jnp.float32)


def on_device(
    hidden_in,
    boundary,
    norm_gain,
    proj_weight,
    rate_weight,
    conv_weight,
    log_rate,
    rate_bias,
    head_gain,
    out_weight,
    ffn_norm_gain,
    gate_up_weight,
    down_weight,
    grad_out,
):
    own = hidden_in.shape[1]
    seq = lax.axis_size("seq")
    split = 2 * seq
    length = own * seq
    tokens = 2 * length
    heads = HEADS // split
    hk, hv, ff = heads * KEY, heads * VALUE, FF // split
    chan = 2 * hk + hv
    here = lax.axis_index("core") * seq + lax.axis_index("seq")

    mix_in = weight_columns(
        [proj_weight[:, :HK], proj_weight[:, HK : 2 * HK], proj_weight[:, 2 * HK : 2 * HK + HV]],
        split,
    )
    rate_all = lax.all_gather(rate_weight, ("z", "core", "seq"), axis=0, tiled=True)
    gate_out = weight_columns([proj_weight[:, 2 * HK + HV :], out_weight], split)
    gate_in, out_cols = gate_out[:, :hv], gate_out[:, hv:]
    ffn_in = weight_columns([gate_up_weight[:, :FF], gate_up_weight[:, FF:]], split)
    down_cols = weight_columns([down_weight], split)

    x = hidden_in[0].astype(jnp.float32)
    scale = lax.rsqrt(jnp.mean(x * x, axis=1, keepdims=True) + EPS)
    normed = x * scale
    first_in = plane_gather((normed * norm_gain).astype(jnp.bfloat16))
    cot = plane_gather(grad_out[0])

    bounds = boundary
    other = swap_core(bounds)
    core = lax.axis_index("core")
    bounds = jnp.where(
        core == 0, jnp.concatenate([bounds, other], 0), jnp.concatenate([other, bounds], 0)
    )
    positions = jnp.arange(length)
    start = jnp.logical_or(
        jnp.any(positions[None, :, None] == bounds[:, None, :], axis=2), positions == 0
    ).astype(jnp.float32)

    projected = jnp.dot(first_in, mix_in, preferred_element_type=jnp.float32)
    rates = jnp.dot(first_in, rate_all, preferred_element_type=jnp.float32)
    conv_in = projected.astype(jnp.bfloat16).astype(jnp.float32).reshape(2, length, chan)

    def own_columns(whole, width):
        return lax.dynamic_slice_in_dim(whole, here * width, width, whole.ndim - 1)

    taps = jnp.concatenate(
        [
            own_columns(conv_weight[:, :HK], hk),
            own_columns(conv_weight[:, HK : 2 * HK], hk),
            own_columns(conv_weight[:, 2 * HK :], hv),
        ],
        axis=1,
    )
    conv_out = taps[CONV - 1] * conv_in
    keep = jnp.ones((2, length), jnp.float32)
    keeps = [keep]
    for lag in range(1, CONV):
        before = jnp.pad(start, ((0, 0), (lag - 1, 0)))[:, :length]
        keep = keep * (1.0 - before)
        keeps.append(keep)
        moved = jnp.pad(conv_in, ((0, 0), (lag, 0), (0, 0)))[:, :length]
        conv_out = conv_out + taps[CONV - 1 - lag] * moved * keep[:, :, None]
    act = jax.nn.silu(conv_out)
    query_raw = act[:, :, :hk].reshape(2, length, heads, KEY)
    key_raw = act[:, :, hk : 2 * hk].reshape(2, length, heads, KEY)
    query_factor = lax.rsqrt(jnp.sum(query_raw * query_raw, axis=3, keepdims=True) + EPS)
    key_factor = lax.rsqrt(jnp.sum(key_raw * key_raw, axis=3, keepdims=True) + EPS)
    query_unit = query_raw * query_factor
    key_unit = key_raw * key_factor
    query = rounded(query_unit * KEY ** (-0.5))
    keys = rounded(key_unit)
    values = rounded(act[:, :, 2 * hk :].reshape(2, length, heads, VALUE))
    own_rate, own_bias = own_columns(log_rate, heads), own_columns(rate_bias, heads)
    rate_input = own_columns(rates[:, :HEADS], heads).reshape(2, length, heads) + own_bias
    decay_log = -jnp.exp(own_rate) * jax.nn.softplus(rate_input)
    beta = jax.nn.sigmoid(own_columns(rates[:, HEADS:], heads)).reshape(2, length, heads)
    state_zero = jnp.zeros((2, heads, VALUE, KEY), jnp.float32)

    def recur(query_in, keys_in, values_in, decay_in, beta_in):
        def one(state, q, k, v, d, b, s):
            return seq_pass(state, q, k, v, d, b, s, GROUP)

        return jax.vmap(one)(state_zero, query_in, keys_in, values_in, decay_in, beta_in, start)

    (final, mixed), pullback = jax.vjp(recur, query, keys, values, decay_log, beta)

    gate_view = jnp.dot(first_in, gate_in, preferred_element_type=jnp.float32).reshape(
        2, length, heads, VALUE
    )
    head_factor = lax.rsqrt(jnp.mean(mixed * mixed, axis=3, keepdims=True) + EPS)
    head_unit = mixed * head_factor
    gate_act = jax.nn.silu(gate_view)
    branch = (head_unit * head_gain * gate_act).reshape(tokens, hv).astype(jnp.bfloat16)
    hidden = x + plane_sum(contract_rows(branch, out_cols))
    scale_two = lax.rsqrt(jnp.mean(hidden * hidden, axis=1, keepdims=True) + EPS)
    normed_two = hidden * scale_two
    second_in = plane_gather((normed_two * ffn_norm_gain).astype(jnp.bfloat16))
    both = jnp.dot(second_in, ffn_in, preferred_element_type=jnp.float32)
    gate_part = both[:, :ff]
    up_part = both[:, ff:]
    gate_silu = jax.nn.silu(gate_part)
    inner = (gate_silu * up_part).astype(jnp.bfloat16)
    result = hidden + plane_sum(contract_rows(inner, down_cols))

    d_inner = jnp.dot(cot, down_cols, preferred_element_type=jnp.float32)
    d_both = jnp.concatenate(
        [d_inner * up_part * silu_slope(gate_part), d_inner * gate_silu], axis=1
    ).astype(jnp.bfloat16)
    d_second = plane_sum(contract_rows(d_both, ffn_in))
    grad_ffn_in = weight_rows(contract_tokens(second_in, d_both), split)
    grad_down = weight_rows(contract_tokens(cot, inner), split)
    grad_gain_two = jnp.sum(d_second * normed_two, axis=0)
    d_hidden = grad_out[0].astype(jnp.float32) + norm_back(
        normed_two, scale_two, d_second * ffn_norm_gain
    )
    d_mix = plane_gather(d_hidden.astype(jnp.bfloat16))
    d_branch = jnp.dot(d_mix, out_cols, preferred_element_type=jnp.float32).reshape(
        2, length, heads, VALUE
    )
    d_scaled = d_branch * gate_act
    grad_head_gain = jnp.sum(d_scaled * head_unit, axis=(0, 1, 2))
    d_gate = (
        (d_branch * head_unit * head_gain * silu_slope(gate_view))
        .reshape(tokens, hv)
        .astype(jnp.bfloat16)
    )
    d_mixed = norm_back(head_unit, head_factor, d_scaled * head_gain)
    grad_gate_out = weight_rows(
        jnp.concatenate([contract_tokens(first_in, d_gate), contract_tokens(d_mix, branch)], 1),
        split,
    )
    d_query, d_keys, d_values, d_decay, d_beta = pullback((state_zero, d_mixed))
    d_query, d_keys, d_values = rounded(d_query), rounded(d_keys), rounded(d_values)
    d_query_raw = unit_back(query_unit, query_factor, d_query * KEY ** (-0.5))
    d_key_raw = unit_back(key_unit, key_factor, d_keys)
    d_act = jnp.concatenate(
        [
            d_query_raw.reshape(2, length, hk),
            d_key_raw.reshape(2, length, hk),
            d_values.reshape(2, length, hv),
        ],
        axis=2,
    )
    d_conv = d_act * silu_slope(conv_out)
    d_conv_in = taps[CONV - 1] * d_conv
    tap_grads = [None] * CONV
    tap_grads[CONV - 1] = jnp.sum(d_conv * conv_in, axis=(0, 1))
    for lag in range(1, CONV):
        masked = d_conv * keeps[lag][:, :, None]
        moved = jnp.pad(conv_in, ((0, 0), (lag, 0), (0, 0)))[:, :length]
        tap_grads[CONV - 1 - lag] = jnp.sum(masked * moved, axis=(0, 1))
        d_conv_in = d_conv_in + taps[CONV - 1 - lag] * jnp.pad(
            masked, ((0, 0), (0, lag), (0, 0))
        )[:, lag:]
    grad_taps = jnp.stack(tap_grads, axis=0)
    d_rate_input = d_decay * -jnp.exp(own_rate) * jax.nn.sigmoid(rate_input)
    grad_log_rate = jnp.sum(d_decay * decay_log, axis=(0, 1))
    grad_rate_bias = jnp.sum(d_rate_input, axis=(0, 1))
    d_rates = jnp.concatenate(
        [d_rate_input, d_beta * beta * (1.0 - beta)], axis=2
    ).astype(jnp.bfloat16).reshape(tokens, 2 * heads)
    rate_cols = jnp.concatenate(
        [own_columns(rate_all[:, :HEADS], heads), own_columns(rate_all[:, HEADS:], heads)], axis=1
    )
    d_conv_low = d_conv_in.reshape(tokens, chan).astype(jnp.bfloat16)
    d_first = plane_sum(
        contract_rows(d_conv_low, mix_in)
        + contract_rows(d_gate, gate_in)
        + contract_rows(d_rates, rate_cols)
    )
    grad_mix_in = weight_rows(contract_tokens(first_in, d_conv_low), split)
    grad_gain_one = jnp.sum(d_first * normed, axis=0)
    d_row = d_hidden + norm_back(normed, scale, d_first * norm_gain)

    grad_rate = contract_tokens(first_in, d_rates)
    sides = jnp.concatenate(
        [grad_taps.reshape(-1), grad_log_rate, grad_rate_bias, grad_rate.reshape(-1)]
    )
    sums = jnp.concatenate([grad_gain_one, grad_gain_two, grad_head_gain])
    n_sides = sides.shape[0]
    small = lax.psum(jnp.concatenate([sides, sums]), "z")
    small = lax.all_gather(small, PLANE, axis=0)
    sums = jnp.sum(small[:, n_sides:], axis=0)
    width = norm_gain.shape[0]

    def side(at, count):
        return small[:, at : at + count]

    grad_conv = side(0, CONV * chan).reshape(split, CONV, chan)
    grad_conv = jnp.swapaxes(grad_conv, 0, 1)
    grad_conv = jnp.concatenate(
        [
            grad_conv[:, :, :hk].reshape(CONV, HK),
            grad_conv[:, :, hk : 2 * hk].reshape(CONV, HK),
            grad_conv[:, :, 2 * hk :].reshape(CONV, HV),
        ],
        axis=1,
    )
    at = CONV * chan
    grad_log_rate = side(at, heads).reshape(HEADS)
    grad_rate_bias = side(at + heads, heads).reshape(HEADS)
    rows = proj_weight.shape[0]
    first_row = (lax.axis_index("z") * split + here) * rows
    grad_rate = lax.dynamic_slice_in_dim(
        side(at + 2 * heads, width * 2 * heads).reshape(split, width, 2 * heads), first_row, rows, 1
    )
    grad_rate = jnp.concatenate(
        [
            jnp.swapaxes(grad_rate[:, :, :heads], 0, 1).reshape(rows, HEADS),
            jnp.swapaxes(grad_rate[:, :, heads:], 0, 1).reshape(rows, HEADS),
        ],
        axis=1,
    )
    grad_proj = jnp.concatenate(
        [
            grad_mix_in[:, :, :hk].reshape(rows, HK),
            grad_mix_in[:, :, hk : 2 * hk].reshape(rows, HK),
            grad_mix_in[:, :, 2 * hk :].reshape(rows, HV),
            grad_gate_out[:, :, :hv].reshape(rows, HV),
        ],
        axis=1,
    )
    grad_gate_up = jnp.concatenate(
        [grad_ffn_in[:, :, :ff].reshape(rows, FF), grad_ffn_in[:, :, ff:].reshape(rows, FF)], axis=1
    )
    finals = lax.all_gather(final, PLANE, axis=0)
    final_state = lax.dynamic_index_in_dim(finals, core, 1, keepdims=False)
    final_state = final_state.reshape(HEADS, VALUE, KEY)
    return (
        result.astype(jnp.bfloat16)[None],
        d_row.astype(jnp.bfloat16)[None],
        final_state[None],
        sums[:width],
        grad_proj,
        grad_rate,
        grad_conv,
        grad_log_rate,
        grad_rate_bias,
        sums[2 * width :],
        grad_gate_out[:, :, hv:].reshape(rows, HV),
        sums[width : 2 * width],
        grad_gate_up,
        grad_down.reshape(rows, FF),
    )


def solution(mesh):
    dp, seq = mesh.shape["dp"], mesh.shape["seq"]
    planes = Mesh(mesh.devices.reshape(dp // 2, 2, seq), ("z", "core", "seq"))
    row = ("z", "core")
    every = ("z", "core", "seq")
    in_specs = (
        P(row, "seq", None),
        P(row, None),
        P(),
        P(every, None),
        P(every, None),
        P(),
        P(),
        P(),
        P(),
        P(every, None),
        P(),
        P(every, None),
        P(every, None),
        P(row, "seq", None),
    )
    out_specs = (
        P(row, "seq", None),
        P(row, "seq", None),
        P(row, None, None, None),
        P(),
        P(every, None),
        P(every, None),
        P(),
        P(),
        P(),
        P(),
        P(every, None),
        P(),
        P(every, None),
        P(every, None),
    )
    return jax.shard_map(
        on_device, mesh=planes, in_specs=in_specs, out_specs=out_specs, check_vma=False
    )
```

```python
import functools

import jax
import jax.numpy as jnp
from jax import lax
from jax.experimental import pallas as pl
from jax.experimental.pallas import tpu as pltpu
from jax.sharding import Mesh
from jax.sharding import PartitionSpec as P

HEADS = 16
FF = 5504
HK = 2048
HV = 4096
PLANE = ("core", "seq")
KEY = 128
VALUE = 256
CONV = 4
EPS = 1e-06
BLOCK = 128
F32 = jnp.float32
LOW = jnp.bfloat16


def halves(x):
    high = x.astype(LOW)
    return (high, (x - high.astype(F32)).astype(LOW))


def thirds(x):
    high = x.astype(LOW)
    rest = x - high.astype(F32)
    middle = rest.astype(LOW)
    return (high, middle, (rest - middle.astype(F32)).astype(LOW))


def product(left, right, left_dim=1, right_dim=0):
    total = None
    for i, a in enumerate(left):
        for j, b in enumerate(right):
            if i + j < max(len(left), len(right)):
                term = lax.dot_general(
                    a, b, (((left_dim,), (right_dim,)), ((), ())), preferred_element_type=F32
                )
                total = term if total is None else total + term
    return total


def places():
    row = lax.broadcasted_iota(jnp.int32, (BLOCK, BLOCK), 0)
    col = lax.broadcasted_iota(jnp.int32, (BLOCK, BLOCK), 1)
    return row, col


def running(aux, row, col):
    lower = (row >= col).astype(LOW)
    return product((lower,), thirds(aux))


def solved(negated, row, col):
    diagonal = jnp.where((row >> 4) == (col >> 4), negated, 0.0)
    inverse = (row == col).astype(F32) + diagonal
    power = diagonal
    for _ in range(3):
        parts = halves(power)
        power = product(parts, parts)
        inverse = inverse + product(halves(inverse), halves(power))
    for bits in (4, 5, 6):
        beside = jnp.logical_and(
            (row >> (bits + 1)) == (col >> (bits + 1)), (row >> bits) != (col >> bits)
        )
        off = jnp.where(beside, negated, 0.0)
        parts = halves(inverse)
        inverse = inverse + product(parts, halves(product(halves(off), parts)))
    return inverse


def decays(aux, row, col, heads):
    sums = running(aux, row, col)
    turned = sums.T
    aux_turned = aux.T
    seg_col, seg_row = sums[:, 2 * heads : 2 * heads + 1], turned[2 * heads : 2 * heads + 1, :]
    joined = jnp.logical_and(row >= col, seg_col == seg_row)
    seg_last = sums[BLOCK - 1 :, 2 * heads : 2 * heads + 1]
    out = []
    for h in range(heads):
        g_col, g_row = sums[:, h : h + 1], turned[h : h + 1, :]
        pair = jnp.where(joined, jnp.exp(jnp.where(joined, g_col - g_row, 0.0)), 0.0)
        alive_col = jnp.where(seg_col == 0.0, jnp.exp(g_col), 0.0)
        alive_row = jnp.where(seg_row == 0.0, jnp.exp(g_row), 0.0)
        last = jnp.where(seg_col == seg_last, jnp.exp(sums[BLOCK - 1 :, h : h + 1] - g_col), 0.0)
        out.append(
            dict(
                pair=pair,
                decay_col=alive_col,
                decay_row=alive_row,
                decay_last=alive_col[BLOCK - 1 :, :],
                last=last,
                beta_col=aux[:, heads + h : heads + h + 1],
                beta_row=aux_turned[heads + h : heads + h + 1, :],
            )
        )
    return out


def convolved(ext, taps, aux, heads):
    total = taps[CONV - 1 : CONV, :] * ext(0)
    for lag in range(1, CONV):
        keep = aux[:, 2 * heads + lag : 2 * heads + lag + 1]
        total = total + taps[CONV - 1 - lag : CONV - lag, :] * (ext(lag) * keep)
    return total


def unit(raw):
    factor = lax.rsqrt(jnp.sum(raw * raw, axis=1, keepdims=True) + EPS)
    return raw * factor, factor


def mix_kernel(
    heads, x_ref, taps_ref, aux_ref, mixed_ref, inv_ref, upd_ref, state_ref, final_ref, ext, state
):
    step = pl.program_id(0)
    hk = heads * KEY
    row, col = places()

    @pl.when(step == 0)
    def _():
        state[...] = jnp.zeros_like(state)
        ext[:, :8, :] = jnp.zeros_like(ext[:, :8, :])

    state_ref[0] = state[...]
    taps = taps_ref[...]
    for r in range(2):
        aux = aux_ref[r]
        ext[r, 8:, :] = x_ref[r].astype(F32)
        conv = convolved(lambda lag: ext[r, 8 - lag : 8 - lag + BLOCK, :], taps, aux, heads)
        act = conv * jax.nn.sigmoid(conv)
        ext[r, :8, :] = ext[r, BLOCK:, :]
        facts = decays(aux, row, col, heads)
        for h in range(heads):
            f = facts[h]
            at = r * heads + h
            vs = slice(h * VALUE, (h + 1) * VALUE)
            query = (unit(act[:, h * KEY : (h + 1) * KEY])[0] * KEY ** (-0.5)).astype(LOW)
            keys = unit(act[:, hk + h * KEY : hk + (h + 1) * KEY])[0].astype(LOW)
            values = act[:, 2 * hk + h * VALUE : 2 * hk + (h + 1) * VALUE].astype(LOW)
            pair = f["pair"]
            similar = product((keys,), (keys,), 1, 1)
            negated = jnp.where(row > col, -(f["beta_col"] * pair * similar), 0.0)
            inverse = solved(negated, row, col)
            inv_ref[0, at] = inverse
            scaled = inverse * f["beta_row"]
            old = state[at]
            old_parts = halves(old)
            weights = halves(product(halves(scaled * f["decay_row"]), (keys,)))
            updates = product(halves(scaled), (values,)) - product(weights, old_parts)
            upd_ref[r, :, vs] = updates
            seen = product((query,), (keys,), 1, 1) * pair
            mixed_ref[r, :, vs] = f["decay_col"] * product((query,), old_parts) + product(
                halves(seen), halves(updates)
            )
            state[at] = f["decay_last"] * old + product(
                (keys,), halves(f["last"] * updates), 0, 0
            )

    @pl.when(step == pl.num_programs(0) - 1)
    def _():
        for at in range(2 * heads):
            final_ref[at] = state[at].T


def mix(x, taps, aux, heads):
    length, chan = x.shape[1:]
    count = length // BLOCK
    hv = heads * VALUE
    here = lambda j: (0, j, 0)
    saved = lambda j: (j, 0, 0, 0)
    return pl.pallas_call(
        functools.partial(mix_kernel, heads),
        grid=(count,),
        in_specs=[
            pl.BlockSpec((2, BLOCK, chan), here),
            pl.BlockSpec((CONV, chan), lambda j: (0, 0)),
            pl.BlockSpec((2, BLOCK, 128), here),
        ],
        out_specs=[
            pl.BlockSpec((2, BLOCK, hv), here),
            pl.BlockSpec((1, 2 * heads, BLOCK, BLOCK), saved),
            pl.BlockSpec((2, BLOCK, hv), here),
            pl.BlockSpec((1, 2 * heads, KEY, VALUE), saved),
            pl.BlockSpec((2 * heads, VALUE, KEY), lambda j: (0, 0, 0)),
        ],
        out_shape=[
            jax.ShapeDtypeStruct((2, length, hv), F32),
            jax.ShapeDtypeStruct((count, 2 * heads, BLOCK, BLOCK), F32),
            jax.ShapeDtypeStruct((2, length, hv), F32),
            jax.ShapeDtypeStruct((count, 2 * heads, KEY, VALUE), F32),
            jax.ShapeDtypeStruct((2 * heads, VALUE, KEY), F32),
        ],
        scratch_shapes=[
            pltpu.VMEM((2, BLOCK + 8, chan), F32),
            pltpu.VMEM((2 * heads, KEY, VALUE), F32),
        ],
        compiler_params=pltpu.CompilerParams(
            dimension_semantics=("arbitrary",), vmem_limit_bytes=48 * 1024 * 1024
        ),
        cost_estimate=pl.CostEstimate(
            flops=40_000_000_000, bytes_accessed=12_000_000, transcendentals=2_000_000
        ),
        name="mix_forward",
    )(x, taps, aux)


def slope(value):
    logistic = jax.nn.sigmoid(value)
    return logistic, logistic * (1.0 + value * (1.0 - logistic))


def mix_back_kernel(
    heads,
    x_ref,
    halo_ref,
    taps_ref,
    aux_ref,
    gate_ref,
    gain_ref,
    mixed_ref,
    inv_ref,
    upd_ref,
    state_ref,
    d_branch_ref,
    d_x_ref,
    d_gate_ref,
    d_aux_ref,
    d_taps_ref,
    d_gain_ref,
    ext,
    d_ext,
    d_state,
):
    step = pl.program_id(0)
    first_block = step == pl.num_programs(0) - 1
    hk = heads * KEY
    row, col = places()
    lane = lax.broadcasted_iota(jnp.int32, (BLOCK, 128), 1)
    position = lax.broadcasted_iota(jnp.int32, (BLOCK, 1), 0)

    @pl.when(step == 0)
    def _():
        d_state[...] = jnp.zeros_like(d_state)
        d_ext[:, BLOCK:, :] = jnp.zeros_like(d_ext[:, BLOCK:, :])
        d_taps_ref[...] = jnp.zeros_like(d_taps_ref)
        d_gain_ref[...] = jnp.zeros_like(d_gain_ref)

    taps = taps_ref[...]
    gain = gain_ref[...]
    for r in range(2):
        aux = aux_ref[r]
        before = halo_ref[r][8:, :].astype(F32)
        ext[r, :8, :] = jnp.where(first_block, 0.0, before)
        ext[r, 8:, :] = x_ref[r].astype(F32)
        shifted = lambda lag: ext[r, 8 - lag : 8 - lag + BLOCK, :]
        conv = convolved(shifted, taps, aux, heads)
        logistic, conv_slope = slope(conv)
        act = conv * logistic
        facts = decays(aux, row, col, heads)
        columns = jnp.zeros((BLOCK, 128), F32)
        rows = []
        d_query_raw, d_key_raw, d_value_raw = [], [], []
        d_betas = []
        for h in range(heads):
            f = facts[h]
            at = r * heads + h
            vs = slice(h * VALUE, (h + 1) * VALUE)
            query_unit, query_factor = unit(act[:, h * KEY : (h + 1) * KEY])
            key_unit, key_factor = unit(act[:, hk + h * KEY : hk + (h + 1) * KEY])
            query = (query_unit * KEY ** (-0.5)).astype(LOW)
            keys = key_unit.astype(LOW)
            values = act[:, 2 * hk + h * VALUE : 2 * hk + (h + 1) * VALUE].astype(LOW)
            mixed = mixed_ref[r, :, vs]
            gate = gate_ref[r, :, vs]
            d_branch = d_branch_ref[r, :, vs]
            factor = lax.rsqrt(jnp.mean(mixed * mixed, axis=1, keepdims=True) + EPS)
            normed = mixed * factor
            gate_logistic, gate_slope = slope(gate)
            d_scaled = d_branch * (gate * gate_logistic)
            d_gain_ref[...] += jnp.sum(d_scaled * normed, axis=0, keepdims=True)
            d_gate_ref[r, :, vs] = (d_branch * normed * gain * gate_slope).astype(LOW)
            d_normed = d_scaled * gain
            d_out = factor * (
                d_normed - normed * jnp.mean(d_normed * normed, axis=1, keepdims=True)
            )
            pair, beta, decay = f["pair"], f["beta_col"], f["decay_col"]
            inverse, updates, old = halves(inv_ref[0, at]), upd_ref[r, :, vs], state_ref[0, at]
            upd_parts, old_parts, out_parts = halves(updates), halves(old), halves(d_out)
            d_new = d_state[at]
            d_new_parts = halves(d_new)
            similar = product((keys,), (keys,), 1, 1)
            seen = product((query,), (keys,), 1, 1) * pair
            carried = product((keys,), d_new_parts)
            d_updates = product(halves(seen), out_parts, 0, 0) + f["last"] * carried
            d_targets = product(inverse, halves(d_updates), 0, 0)
            target_parts = halves(d_targets)
            below = jnp.where(row > col, -product(target_parts, upd_parts, 1, 1), 0.0)
            d_seen = product(out_parts, upd_parts, 1, 1)
            below_pair = below * pair
            d_similar = halves(below_pair * beta)
            d_seen_pair = halves(d_seen * pair)
            target_state = product(target_parts, old_parts, 1, 1)
            out_state = product(out_parts, old_parts, 1, 1)
            keys_wide, query_wide = keys.astype(F32), query.astype(F32)
            d_query = decay * out_state + product(d_seen_pair, (keys,))
            d_keys = (
                product(d_similar, (keys,))
                + product(d_similar, (keys,), 0, 0)
                + product(d_seen_pair, (query,), 0, 0)
                + f["last"] * product(upd_parts, d_new_parts, 1, 1)
                - (beta * decay) * target_state
            )
            d_values = beta * d_targets
            key_target = jnp.sum(keys_wide * target_state, axis=1, keepdims=True)
            by_beta = below_pair * similar
            d_beta = (
                jnp.sum(d_targets * values.astype(F32), axis=1, keepdims=True)
                - decay * key_target
                + jnp.sum(by_beta, axis=1, keepdims=True)
            )
            d_pair = by_beta * beta + d_seen * seen
            d_decay = jnp.sum(query_wide * out_state, axis=1, keepdims=True) - beta * key_target
            d_last = f["last"] * jnp.sum(updates * carried, axis=1, keepdims=True)
            at_last = jnp.sum(d_last, axis=0, keepdims=True) + f["decay_last"] * jnp.sum(
                jnp.sum(d_new * old, axis=1, keepdims=True), axis=0, keepdims=True
            )
            d_sums = (
                jnp.sum(d_pair, axis=1, keepdims=True)
                + decay * d_decay
                - d_last
                + jnp.where(position == BLOCK - 1, at_last, 0.0)
            )
            columns = jnp.where(lane == h, d_sums, columns)
            rows.append(jnp.sum(d_pair, axis=0, keepdims=True))
            d_betas.append(d_beta)
            d_state[at] = (
                f["decay_last"] * d_new
                + product((query,), halves(decay * d_out), 0, 0)
                - product((keys,), halves((beta * decay) * d_targets), 0, 0)
            )
            d_query = d_query.astype(LOW).astype(F32) * KEY ** (-0.5)
            d_keys = d_keys.astype(LOW).astype(F32)
            d_query_raw.append(
                query_factor
                * (d_query - query_unit * jnp.sum(d_query * query_unit, axis=1, keepdims=True))
            )
            d_key_raw.append(
                key_factor * (d_keys - key_unit * jnp.sum(d_keys * key_unit, axis=1, keepdims=True))
            )
            d_value_raw.append(d_values.astype(LOW).astype(F32))
        turned = jnp.concatenate(
            rows + [jnp.zeros((128 - heads, BLOCK), F32)], axis=0
        ).T
        upper = (row <= col).astype(LOW)
        d_aux = product((upper,), thirds(columns - turned))
        for h in range(heads):
            d_aux = jnp.where(lane == heads + h, d_betas[h], d_aux)
        d_aux_ref[r] = d_aux
        d_conv = jnp.concatenate(d_query_raw + d_key_raw + d_value_raw, axis=1) * conv_slope
        d_ext_sum = taps[CONV - 1 : CONV, :] * d_conv
        d_taps_ref[CONV - 1 : CONV, :] += jnp.sum(d_conv * shifted(0), axis=0, keepdims=True)
        for lag in range(1, CONV):
            masked = d_conv * aux[:, 2 * heads + lag : 2 * heads + lag + 1]
            d_taps_ref[CONV - 1 - lag : CONV - lag, :] += jnp.sum(
                masked * shifted(lag), axis=0, keepdims=True
            )
            slot = r * (CONV - 1) + lag - 1
            d_ext[slot, :BLOCK, :] = masked
            d_ext_sum = (
                d_ext_sum + taps[CONV - 1 - lag : CONV - lag, :] * d_ext[slot, lag : lag + BLOCK, :]
            )
            d_ext[slot, BLOCK:, :] = d_ext[slot, :8, :]
        d_x_ref[r] = d_ext_sum.astype(LOW)


def mix_back(x, taps, aux, gate, gain, mixed, inverses, updates, states, d_branch, heads):
    length, chan = x.shape[1:]
    count = length // BLOCK
    hv = heads * VALUE
    here = lambda j: (0, count - 1 - j, 0)
    halo = lambda j: (0, jnp.maximum((count - 1 - j) * (BLOCK // 16) - 1, 0), 0)
    saved = lambda j: (count - 1 - j, 0, 0, 0)
    fixed = lambda j: (0, 0)
    return pl.pallas_call(
        functools.partial(mix_back_kernel, heads),
        grid=(count,),
        in_specs=[
            pl.BlockSpec((2, BLOCK, chan), here),
            pl.BlockSpec((2, 16, chan), halo),
            pl.BlockSpec((CONV, chan), fixed),
            pl.BlockSpec((2, BLOCK, 128), here),
            pl.BlockSpec((2, BLOCK, hv), here),
            pl.BlockSpec((1, VALUE), fixed),
            pl.BlockSpec((2, BLOCK, hv), here),
            pl.BlockSpec((1, 2 * heads, BLOCK, BLOCK), saved),
            pl.BlockSpec((2, BLOCK, hv), here),
            pl.BlockSpec((1, 2 * heads, KEY, VALUE), saved),
            pl.BlockSpec((2, BLOCK, hv), here),
        ],
        out_specs=[
            pl.BlockSpec((2, BLOCK, chan), here),
            pl.BlockSpec((2, BLOCK, hv), here),
            pl.BlockSpec((2, BLOCK, 128), here),
            pl.BlockSpec((CONV, chan), fixed),
            pl.BlockSpec((1, VALUE), fixed),
        ],
        out_shape=[
            jax.ShapeDtypeStruct((2, length, chan), LOW),
            jax.ShapeDtypeStruct((2, length, hv), LOW),
            jax.ShapeDtypeStruct((2, length, 128), F32),
            jax.ShapeDtypeStruct((CONV, chan), F32),
            jax.ShapeDtypeStruct((1, VALUE), F32),
        ],
        scratch_shapes=[
            pltpu.VMEM((2, BLOCK + 8, chan), F32),
            pltpu.VMEM((2 * (CONV - 1), BLOCK + 8, chan), F32),
            pltpu.VMEM((2 * heads, KEY, VALUE), F32),
        ],
        compiler_params=pltpu.CompilerParams(
            dimension_semantics=("arbitrary",), vmem_limit_bytes=48 * 1024 * 1024
        ),
        cost_estimate=pl.CostEstimate(
            flops=60_000_000_000, bytes_accessed=20_000_000, transcendentals=4_000_000
        ),
        name="mix_backward",
    )(x, x, taps, aux, gate, gain, mixed, inverses, updates, states, d_branch)


def contract_rows(left, right):
    return lax.dot_general(
        left, right, (((1,), (1,)), ((), ())), preferred_element_type=jnp.float32
    )


def contract_tokens(left, right):
    return lax.dot_general(
        left, right, (((0,), (0,)), ((), ())), preferred_element_type=jnp.float32
    )


def silu_slope(value):
    logistic = jax.nn.sigmoid(value)
    return logistic * (1.0 + value * (1.0 - logistic))


def norm_back(normed, factor, grad):
    return factor * (grad - normed * jnp.mean(grad * normed, axis=-1, keepdims=True))


def swap_core(x):
    return lax.ppermute(x, "core", [(0, 1), (1, 0)])


def from_peer(x, axis, distance):
    return lax.ppermute(x, axis, [(i, i ^ distance) for i in range(lax.axis_size(axis))])


def plane_gather(x, ordered):
    size, me = lax.axis_size("seq"), lax.axis_index("seq")
    blocks = [x] + [from_peer(x, "seq", k) for k in range(1, size)]
    others = [swap_core(b) for b in blocks]
    if not ordered:
        return jnp.concatenate(blocks + others, axis=0)
    tokens = x.shape[0]
    whole = jnp.zeros((2 * size * tokens,) + x.shape[1:], x.dtype)
    for k in range(size):
        whole = lax.dynamic_update_slice(whole, blocks[k], ((me ^ k) * tokens, 0))
        whole = lax.dynamic_update_slice(whole, others[k], ((size + (me ^ k)) * tokens, 0))
    return whole


def plane_sum(x, ordered):
    size, me = lax.axis_size("seq"), lax.axis_index("seq")
    half = x.shape[0] // 2
    tokens = half // size
    row = x[:half] + swap_core(x[half:].astype(jnp.bfloat16)).astype(jnp.float32)

    def block(k):
        at = (me ^ k) * tokens if ordered else k * tokens
        return lax.dynamic_slice_in_dim(row, at, tokens, 0)

    total = block(0)
    for k in range(1, size):
        total = total + from_peer(block(k).astype(jnp.bfloat16), "seq", k).astype(jnp.float32)
    return total


def by_holder(parts, split):
    rows = parts[0].shape[0]
    return jnp.concatenate(
        [jnp.swapaxes(p.reshape(rows, split, -1), 0, 1) for p in parts], axis=2
    )


def plane_exchange(blocks):
    got = lax.all_to_all(blocks, PLANE, 0, 0)
    return got.reshape(-1, got.shape[2])


def along_z(x):
    return lax.all_gather(x, "z", axis=0, tiled=True)


def shard_sum(partial):
    return lax.psum_scatter(partial, "z", scatter_dimension=0, tiled=True)


def to_holders(mine, split):
    blocks = lax.all_to_all(mine.reshape(split, -1, mine.shape[1]), PLANE, 0, 0)
    return jnp.swapaxes(blocks, 0, 1).astype(jnp.float32)


def butterfly(x, axis):
    distance = 1
    while distance < lax.axis_size(axis):
        x = x + from_peer(x, axis, distance)
        distance *= 2
    return x


def on_device(
    hidden_in,
    boundary,
    norm_gain,
    proj_weight,
    rate_weight,
    conv_weight,
    log_rate,
    rate_bias,
    head_gain,
    out_weight,
    ffn_norm_gain,
    gate_up_weight,
    down_weight,
    grad_out,
):
    own = hidden_in.shape[1]
    width = hidden_in.shape[2]
    seq = lax.axis_size("seq")
    split = 2 * seq
    length = own * seq
    tokens = 2 * length
    heads = HEADS // split
    hk, hv, ff = heads * KEY, heads * VALUE, FF // split
    chan = 2 * hk + hv
    me = lax.axis_index("seq")
    core = lax.axis_index("core")
    here = core * seq + me
    rows = proj_weight.shape[0]

    def own_columns(whole, count):
        return lax.dynamic_slice_in_dim(whole, here * count, count, whole.ndim - 1)

    mix_in = plane_exchange(
        by_holder(
            [
                proj_weight[:, :HK],
                proj_weight[:, HK : 2 * HK],
                proj_weight[:, 2 * HK : 2 * HK + HV],
                rate_weight[:, :HEADS],
                rate_weight[:, HEADS:],
            ],
            split,
        )
    )
    x = hidden_in[0].astype(jnp.float32)
    scale = lax.rsqrt(jnp.mean(x * x, axis=1, keepdims=True) + EPS)
    normed = x * scale
    first_in = plane_gather((normed * norm_gain).astype(jnp.bfloat16), True)
    others = by_holder(
        [
            proj_weight[:, 2 * HK + HV :],
            out_weight,
            gate_up_weight[:, :FF],
            gate_up_weight[:, FF:],
            down_weight,
        ],
        split,
    )
    first_in, others = lax.optimization_barrier((first_in, others))
    others = plane_exchange(others)
    mix_in = along_z(mix_in)
    gate_out = along_z(others[:, : 2 * hv])
    gate_in, out_cols = gate_out[:, :hv], gate_out[:, hv:]
    cut = -(-ff // 256) * 128
    parts = [slice(0, cut), slice(cut, ff)]
    gates = [others[:, 2 * hv :][:, p] for p in parts]
    ups = [others[:, 2 * hv + ff :][:, p] for p in parts]
    downs = [others[:, 2 * hv + 2 * ff :][:, p] for p in parts]
    ffn = [along_z(jnp.concatenate(w, axis=1)) for w in zip(gates, ups, downs)]
    cot = plane_gather(grad_out[0], False)

    bounds = jnp.concatenate([boundary, swap_core(boundary)], axis=0)
    positions = jnp.arange(length)
    start = jnp.logical_or(
        jnp.any(positions[None, :, None] == bounds[:, None, :], axis=2), positions == 0
    ).astype(jnp.float32)
    keep = jnp.ones((2, length), jnp.float32)
    keeps = []
    for lag in range(1, CONV):
        keep = keep * (1.0 - jnp.pad(start, ((0, 0), (lag - 1, 0)))[:, :length])
        keeps.append(keep)
    taps = jnp.concatenate(
        [
            own_columns(conv_weight[:, :HK], hk),
            own_columns(conv_weight[:, HK : 2 * HK], hk),
            own_columns(conv_weight[:, 2 * HK :], hv),
        ],
        axis=1,
    )
    own_rate, own_bias = own_columns(log_rate, heads), own_columns(rate_bias, heads)

    conv_in = jnp.dot(first_in, mix_in[:, :chan], preferred_element_type=jnp.float32)
    conv_in = conv_in.astype(jnp.bfloat16).reshape(2, length, chan)
    rates = jnp.dot(first_in, mix_in[:, chan:], preferred_element_type=jnp.float32)
    rates = rates.reshape(2, length, 2 * heads)
    rate_input = rates[:, :, :heads] + own_bias
    decay_log = -jnp.exp(own_rate) * jax.nn.softplus(rate_input)
    beta = jax.nn.sigmoid(rates[:, :, heads:])
    aux = jnp.concatenate([decay_log, beta] + [s[:, :, None] for s in [start] + keeps], axis=2)
    aux = jnp.pad(aux, ((0, 0), (0, 0), (0, 128 - aux.shape[2])))
    mixed, inverses, updates, states, final = mix(conv_in, taps, aux, heads)

    gate = jnp.dot(first_in, gate_in, preferred_element_type=jnp.float32).reshape(2, length, hv)
    branch = []
    for h in range(heads):
        part = mixed[:, :, h * VALUE : (h + 1) * VALUE]
        factor = lax.rsqrt(jnp.mean(part * part, axis=2, keepdims=True) + EPS)
        branch.append(
            part * factor * head_gain * jax.nn.silu(gate[:, :, h * VALUE : (h + 1) * VALUE])
        )
    branch = jnp.concatenate(branch, axis=2).astype(jnp.bfloat16).reshape(tokens, hv)
    hidden = x + plane_sum(contract_rows(branch, out_cols), True)

    scale_two = lax.rsqrt(jnp.mean(hidden * hidden, axis=1, keepdims=True) + EPS)
    normed_two = hidden * scale_two
    second_in = plane_gather((normed_two * ffn_norm_gain).astype(jnp.bfloat16), False)
    d_second = jnp.zeros((tokens, width), jnp.float32)
    fed = jnp.zeros((tokens, width), jnp.float32)
    grad_ffn = []
    for weight in ffn:
        units = weight.shape[1] // 3
        both_in, down_in = weight[:, : 2 * units], weight[:, 2 * units :]
        both = jnp.dot(second_in, both_in, preferred_element_type=jnp.float32)
        gate_part, up_part = both[:, :units], both[:, units:]
        gate_silu = jax.nn.silu(gate_part)
        inner = (gate_silu * up_part).astype(jnp.bfloat16)
        d_inner = jnp.dot(cot, down_in, preferred_element_type=jnp.float32)
        d_both = jnp.concatenate(
            [d_inner * up_part * silu_slope(gate_part), d_inner * gate_silu], axis=1
        ).astype(jnp.bfloat16)
        d_second = d_second + contract_rows(d_both, both_in)
        fed = fed + contract_rows(inner, down_in)
        grad_ffn.append(
            jnp.concatenate(
                [contract_tokens(second_in, d_both), contract_tokens(cot, inner)], axis=1
            ).astype(jnp.bfloat16)
        )
    grad_ffn[0] = shard_sum(grad_ffn[0])
    grad_ffn[1], grad_ffn[0] = lax.optimization_barrier((grad_ffn[1], grad_ffn[0]))
    grad_ffn[1] = shard_sum(grad_ffn[1])
    d_second = plane_sum(d_second, False)
    result = hidden + plane_sum(fed, False)
    grad_gain_two = jnp.sum(d_second * normed_two, axis=0)
    d_hidden = grad_out[0].astype(jnp.float32) + norm_back(
        normed_two, scale_two, d_second * ffn_norm_gain
    )

    d_mix = plane_gather(d_hidden.astype(jnp.bfloat16), True)
    d_branch = jnp.dot(d_mix, out_cols, preferred_element_type=jnp.float32)
    grad_out_cols = contract_tokens(d_mix, branch).astype(jnp.bfloat16)
    d_branch, grad_ffn[0] = lax.optimization_barrier((d_branch, grad_ffn[0]))
    d_conv_in, d_gate, d_aux, grad_taps, grad_head_gain = mix_back(
        conv_in,
        taps,
        aux,
        gate,
        head_gain[None],
        mixed,
        inverses,
        updates,
        states,
        d_branch.reshape(2, length, hv),
        heads,
    )
    d_conv_in = d_conv_in.reshape(tokens, chan)
    d_gate = d_gate.reshape(tokens, hv)
    d_decay, d_beta = d_aux[:, :, :heads], d_aux[:, :, heads : 2 * heads]
    d_rate_input = d_decay * -jnp.exp(own_rate) * jax.nn.sigmoid(rate_input)
    grad_log_rate = jnp.sum(d_decay * decay_log, axis=(0, 1))
    grad_rate_bias = jnp.sum(d_rate_input, axis=(0, 1))
    d_rates = jnp.concatenate([d_rate_input, d_beta * beta * (1.0 - beta)], axis=2)
    d_rates = d_rates.astype(jnp.bfloat16).reshape(tokens, 2 * heads)
    d_mix_in = jnp.concatenate([d_conv_in, d_rates], axis=1)
    grad_gate_out = jnp.concatenate(
        [contract_tokens(first_in, d_gate).astype(jnp.bfloat16), grad_out_cols], axis=1
    )
    grad_gate_out, grad_ffn[1] = lax.optimization_barrier((grad_gate_out, grad_ffn[1]))
    grad_gate_out = shard_sum(grad_gate_out)
    grad_mix_in = contract_tokens(first_in, d_mix_in).astype(jnp.bfloat16)
    grad_mix_in, grad_gate_out = lax.optimization_barrier((grad_mix_in, grad_gate_out))
    grad_mix_in = to_holders(shard_sum(grad_mix_in), split)
    grad_gate_out = to_holders(grad_gate_out, split)
    grad_ffn = [to_holders(g, split) for g in grad_ffn]
    d_first = contract_rows(d_mix_in, mix_in) + contract_rows(d_gate, gate_in)
    d_first = plane_sum(d_first, True)
    grad_gain_one = jnp.sum(d_first * normed, axis=0)
    d_row = d_hidden + norm_back(normed, scale, d_first * norm_gain)

    sides = jnp.pad(jnp.concatenate([grad_log_rate, grad_rate_bias]), (0, chan - 2 * heads))
    sides = butterfly(jnp.concatenate([grad_taps, sides[None]], axis=0), "z")
    blocks = [sides] + [from_peer(sides, "seq", k) for k in range(1, seq)]
    blocks = [[b, swap_core(b)] for b in blocks]
    sides = jnp.zeros((2, seq) + sides.shape, jnp.float32)
    for k in range(seq):
        for c in range(2):
            sides = lax.dynamic_update_slice(
                sides, blocks[k][c][None, None], (core ^ c, me ^ k, 0, 0)
            )
    sides = sides.reshape(split, CONV + 1, chan)
    grad_conv = jnp.swapaxes(sides[:, :CONV], 0, 1)
    grad_conv = jnp.concatenate(
        [
            grad_conv[:, :, :hk].reshape(CONV, HK),
            grad_conv[:, :, hk : 2 * hk].reshape(CONV, HK),
            grad_conv[:, :, 2 * hk :].reshape(CONV, HV),
        ],
        axis=1,
    )
    sums = jnp.concatenate([grad_gain_one, grad_gain_two, grad_head_gain[0]])
    sums = butterfly(butterfly(butterfly(sums, "core"), "seq"), "z")
    grad_proj = jnp.concatenate(
        [
            grad_mix_in[:, :, :hk].reshape(rows, HK),
            grad_mix_in[:, :, hk : 2 * hk].reshape(rows, HK),
            grad_mix_in[:, :, 2 * hk : chan].reshape(rows, HV),
            grad_gate_out[:, :, :hv].reshape(rows, HV),
        ],
        axis=1,
    )
    grad_rate = jnp.concatenate(
        [
            grad_mix_in[:, :, chan : chan + heads].reshape(rows, HEADS),
            grad_mix_in[:, :, chan + heads :].reshape(rows, HEADS),
        ],
        axis=1,
    )
    units = [g.shape[2] // 3 for g in grad_ffn]

    def hidden_columns(at):
        return jnp.concatenate(
            [g[:, :, at * u : (at + 1) * u] for g, u in zip(grad_ffn, units)], axis=2
        ).reshape(rows, FF)

    grad_gate_up = jnp.concatenate([hidden_columns(0), hidden_columns(1)], axis=1)

    final = final.reshape(2, heads, VALUE, KEY)
    other = swap_core(final[1].astype(jnp.bfloat16))
    pair = jnp.zeros((2, heads, VALUE, KEY), jnp.bfloat16)
    pair = lax.dynamic_update_index_in_dim(pair, final[0].astype(jnp.bfloat16), core, 0)
    pair = lax.dynamic_update_index_in_dim(pair, other, 1 - core, 0)
    final_state = jnp.zeros((2, seq, heads, VALUE, KEY), jnp.float32)
    for k in range(seq):
        block = from_peer(pair, "seq", k) if k else pair
        final_state = lax.dynamic_update_index_in_dim(
            final_state, block.astype(jnp.float32), me ^ k, 1
        )
    return (
        result.astype(jnp.bfloat16)[None],
        d_row.astype(jnp.bfloat16)[None],
        final_state.reshape(1, HEADS, VALUE, KEY),
        sums[:width],
        grad_proj,
        grad_rate,
        grad_conv,
        sides[:, CONV, :heads].reshape(HEADS),
        sides[:, CONV, heads : 2 * heads].reshape(HEADS),
        sums[2 * width :],
        grad_gate_out[:, :, hv:].reshape(rows, HV),
        sums[width : 2 * width],
        grad_gate_up,
        hidden_columns(2),
    )


def solution(mesh):
    dp, seq = mesh.shape["dp"], mesh.shape["seq"]
    planes = Mesh(mesh.devices.reshape(dp // 2, 2, seq), ("z", "core", "seq"))
    row = ("z", "core")
    every = ("z", "core", "seq")
    in_specs = (
        P(row, "seq", None),
        P(row, None),
        P(),
        P(every, None),
        P(every, None),
        P(),
        P(),
        P(),
        P(),
        P(every, None),
        P(),
        P(every, None),
        P(every, None),
        P(row, "seq", None),
    )
    out_specs = (
        P(row, "seq", None),
        P(row, "seq", None),
        P(row, None, None, None),
        P(),
        P(every, None),
        P(every, None),
        P(),
        P(),
        P(),
        P(),
        P(every, None),
        P(),
        P(every, None),
        P(every, None),
    )
    return jax.shard_map(
        on_device, mesh=planes, in_specs=in_specs, out_specs=out_specs, check_vma=False
    )
```

```python
import functools

import jax
import jax.numpy as jnp
from jax import lax
from jax.experimental import pallas as pl
from jax.experimental.pallas import tpu as pltpu
from jax.sharding import Mesh
from jax.sharding import PartitionSpec as P

HEADS = 16
FF = 5504
HK = 2048
HV = 4096
PLANE = ("core", "seq")
KEY = 128
VALUE = 256
CONV = 4
EPS = 1e-06
BLOCK = 128
F32 = jnp.float32
LOW = jnp.bfloat16


def halves(x):
    high = x.astype(LOW)
    return (high, (x - high.astype(F32)).astype(LOW))


def thirds(x):
    high = x.astype(LOW)
    rest = x - high.astype(F32)
    middle = rest.astype(LOW)
    return (high, middle, (rest - middle.astype(F32)).astype(LOW))


def product(left, right, left_dim=1, right_dim=0):
    total = None
    for i, a in enumerate(left):
        for j, b in enumerate(right):
            if i + j < max(len(left), len(right)):
                term = lax.dot_general(
                    a, b, (((left_dim,), (right_dim,)), ((), ())), preferred_element_type=F32
                )
                total = term if total is None else total + term
    return total


def places():
    row = lax.broadcasted_iota(jnp.int32, (BLOCK, BLOCK), 0)
    col = lax.broadcasted_iota(jnp.int32, (BLOCK, BLOCK), 1)
    return row, col


def running(aux, row, col):
    lower = (row >= col).astype(LOW)
    return product((lower,), thirds(aux))


def solved(negated, row, col):
    same = (row >> 4) == (col >> 4)
    power = [jnp.where(same, n, 0.0) for n in negated]
    inverse = [(row == col).astype(F32) + p for p in power]
    for _ in range(3):
        parts = [halves(p) for p in power]
        power = [product(p, p) for p in parts]
        parts = [(halves(i), halves(p)) for i, p in zip(inverse, power)]
        inverse = [i + product(*p) for i, p in zip(inverse, parts)]
    for bits in (4, 5, 6):
        beside = jnp.logical_and(
            (row >> (bits + 1)) == (col >> (bits + 1)), (row >> bits) != (col >> bits)
        )
        off = [halves(jnp.where(beside, n, 0.0)) for n in negated]
        parts = [halves(i) for i in inverse]
        off = [halves(product(o, p)) for o, p in zip(off, parts)]
        inverse = [i + product(p, o) for i, p, o in zip(inverse, parts, off)]
    return inverse


def decays(aux, row, col, heads):
    sums = running(aux, row, col)
    turned = sums.T
    aux_turned = aux.T
    seg_col, seg_row = sums[:, 2 * heads : 2 * heads + 1], turned[2 * heads : 2 * heads + 1, :]
    joined = jnp.logical_and(row >= col, seg_col == seg_row)
    seg_last = sums[BLOCK - 1 :, 2 * heads : 2 * heads + 1]
    out = []
    for h in range(heads):
        g_col, g_row = sums[:, h : h + 1], turned[h : h + 1, :]
        pair = jnp.where(joined, jnp.exp(jnp.where(joined, g_col - g_row, 0.0)), 0.0)
        alive_col = jnp.where(seg_col == 0.0, jnp.exp(g_col), 0.0)
        alive_row = jnp.where(seg_row == 0.0, jnp.exp(g_row), 0.0)
        last = jnp.where(seg_col == seg_last, jnp.exp(sums[BLOCK - 1 :, h : h + 1] - g_col), 0.0)
        out.append(
            dict(
                pair=pair,
                decay_col=alive_col,
                decay_row=alive_row,
                decay_last=alive_col[BLOCK - 1 :, :],
                last=last,
                beta_col=aux[:, heads + h : heads + h + 1],
                beta_row=aux_turned[heads + h : heads + h + 1, :],
            )
        )
    return out


def convolved(ext, taps, aux, heads):
    total = taps[CONV - 1 : CONV, :] * ext(0)
    for lag in range(1, CONV):
        keep = aux[:, 2 * heads + lag : 2 * heads + lag + 1]
        total = total + taps[CONV - 1 - lag : CONV - lag, :] * (ext(lag) * keep)
    return total


def unit(raw):
    factor = lax.rsqrt(jnp.sum(raw * raw, axis=1, keepdims=True) + EPS)
    return raw * factor, factor


def mix_kernel(
    heads, x_ref, taps_ref, aux_ref, mixed_ref, inv_ref, upd_ref, state_ref, final_ref, ext, state
):
    step = pl.program_id(0)
    hk = heads * KEY
    row, col = places()

    @pl.when(step == 0)
    def _():
        state[...] = jnp.zeros_like(state)
        ext[:, :8, :] = jnp.zeros_like(ext[:, :8, :])

    state_ref[0] = state[...]
    taps = taps_ref[...]
    facts, query, keys, values, spans = [], [], [], [], []
    for r in range(2):
        aux = aux_ref[r]
        ext[r, 8:, :] = x_ref[r].astype(F32)
        conv = convolved(lambda lag: ext[r, 8 - lag : 8 - lag + BLOCK, :], taps, aux, heads)
        act = conv * jax.nn.sigmoid(conv)
        ext[r, :8, :] = ext[r, BLOCK:, :]
        facts += decays(aux, row, col, heads)
        for h in range(heads):
            spans.append((r, slice(h * VALUE, (h + 1) * VALUE)))
            query.append(
                (unit(act[:, h * KEY : (h + 1) * KEY])[0] * KEY ** (-0.5)).astype(LOW)
            )
            keys.append(unit(act[:, hk + h * KEY : hk + (h + 1) * KEY])[0].astype(LOW))
            values.append(act[:, 2 * hk + h * VALUE : 2 * hk + (h + 1) * VALUE].astype(LOW))
    every = range(2 * heads)
    similar = [product((k,), (k,), 1, 1) for k in keys]
    inverse = solved(
        [
            jnp.where(row > col, -(f["beta_col"] * f["pair"] * s), 0.0)
            for f, s in zip(facts, similar)
        ],
        row,
        col,
    )
    seen = [product((q,), (k,), 1, 1) * f["pair"] for q, k, f in zip(query, keys, facts)]
    old = [state[at] for at in every]
    old_parts = [halves(o) for o in old]
    asked = [product((q,), o) for q, o in zip(query, old_parts)]
    scaled = [i * f["beta_row"] for i, f in zip(inverse, facts)]
    weights = [
        halves(product(halves(s * f["decay_row"]), (k,))) for s, f, k in zip(scaled, facts, keys)
    ]
    updates = [product(halves(s), (v,)) for s, v in zip(scaled, values)]
    updates = [u - product(w, o) for u, w, o in zip(updates, weights, old_parts)]
    for at in every:
        f, (r, vs) = facts[at], spans[at]
        inv_ref[0, at] = inverse[at]
        upd_ref[r, :, vs] = updates[at]
        state[at] = f["decay_last"] * old[at] + product(
            (keys[at],), halves(f["last"] * updates[at]), 0, 0
        )
    for at in every:
        r, vs = spans[at]
        mixed_ref[r, :, vs] = facts[at]["decay_col"] * asked[at] + product(
            halves(seen[at]), halves(updates[at])
        )

    @pl.when(step == pl.num_programs(0) - 1)
    def _():
        for at in range(2 * heads):
            final_ref[at] = state[at].T


def mix(x, taps, aux, heads):
    length, chan = x.shape[1:]
    count = length // BLOCK
    hv = heads * VALUE
    here = lambda j: (0, j, 0)
    saved = lambda j: (j, 0, 0, 0)
    return pl.pallas_call(
        functools.partial(mix_kernel, heads),
        grid=(count,),
        in_specs=[
            pl.BlockSpec((2, BLOCK, chan), here),
            pl.BlockSpec((CONV, chan), lambda j: (0, 0)),
            pl.BlockSpec((2, BLOCK, 128), here),
        ],
        out_specs=[
            pl.BlockSpec((2, BLOCK, hv), here),
            pl.BlockSpec((1, 2 * heads, BLOCK, BLOCK), saved),
            pl.BlockSpec((2, BLOCK, hv), here),
            pl.BlockSpec((1, 2 * heads, KEY, VALUE), saved),
            pl.BlockSpec((2 * heads, VALUE, KEY), lambda j: (0, 0, 0)),
        ],
        out_shape=[
            jax.ShapeDtypeStruct((2, length, hv), F32),
            jax.ShapeDtypeStruct((count, 2 * heads, BLOCK, BLOCK), F32),
            jax.ShapeDtypeStruct((2, length, hv), F32),
            jax.ShapeDtypeStruct((count, 2 * heads, KEY, VALUE), F32),
            jax.ShapeDtypeStruct((2 * heads, VALUE, KEY), F32),
        ],
        scratch_shapes=[
            pltpu.VMEM((2, BLOCK + 8, chan), F32),
            pltpu.VMEM((2 * heads, KEY, VALUE), F32),
        ],
        compiler_params=pltpu.CompilerParams(
            dimension_semantics=("arbitrary",), vmem_limit_bytes=48 * 1024 * 1024
        ),
        cost_estimate=pl.CostEstimate(
            flops=1_000_000, bytes_accessed=1_000_000, transcendentals=0
        ),
        name="mix_forward",
    )(x, taps, aux)


def slope(value):
    logistic = jax.nn.sigmoid(value)
    return logistic, logistic * (1.0 + value * (1.0 - logistic))


def mix_back_kernel(
    heads,
    x_ref,
    halo_ref,
    taps_ref,
    aux_ref,
    factor_ref,
    gate_ref,
    gain_ref,
    mixed_ref,
    inv_ref,
    upd_ref,
    state_ref,
    d_branch_ref,
    d_all_ref,
    d_taps_ref,
    d_gain_ref,
    d_rate_ref,
    ext,
    d_ext,
    d_state,
):
    step = pl.program_id(0)
    first_block = step == pl.num_programs(0) - 1
    hk, hv = heads * KEY, heads * VALUE
    chan = 2 * hk + hv
    row, col = places()
    lane = lax.broadcasted_iota(jnp.int32, (BLOCK, 128), 1)
    position = lax.broadcasted_iota(jnp.int32, (BLOCK, 1), 0)

    @pl.when(step == 0)
    def _():
        d_state[...] = jnp.zeros_like(d_state)
        d_ext[:, BLOCK:, :] = jnp.zeros_like(d_ext[:, BLOCK:, :])
        d_taps_ref[...] = jnp.zeros_like(d_taps_ref)
        d_gain_ref[...] = jnp.zeros_like(d_gain_ref)
        d_rate_ref[...] = jnp.zeros_like(d_rate_ref)

    taps = taps_ref[...]
    gain = gain_ref[...]
    for r in range(2):
        aux = aux_ref[r]
        before = halo_ref[r][8:, :].astype(F32)
        ext[r, :8, :] = jnp.where(first_block, 0.0, before)
        ext[r, 8:, :] = x_ref[r].astype(F32)
        shifted = lambda lag: ext[r, 8 - lag : 8 - lag + BLOCK, :]
        conv = convolved(shifted, taps, aux, heads)
        logistic, conv_slope = slope(conv)
        act = conv * logistic
        facts = decays(aux, row, col, heads)
        columns = jnp.zeros((BLOCK, 128), F32)
        rows = []
        d_query_raw, d_key_raw, d_value_raw = [], [], []
        d_betas = []
        for h in range(heads):
            f = facts[h]
            at = r * heads + h
            vs = slice(h * VALUE, (h + 1) * VALUE)
            query_unit, query_factor = unit(act[:, h * KEY : (h + 1) * KEY])
            key_unit, key_factor = unit(act[:, hk + h * KEY : hk + (h + 1) * KEY])
            query = (query_unit * KEY ** (-0.5)).astype(LOW)
            keys = key_unit.astype(LOW)
            values = act[:, 2 * hk + h * VALUE : 2 * hk + (h + 1) * VALUE].astype(LOW)
            mixed = mixed_ref[r, :, vs]
            gate = gate_ref[r, :, vs]
            d_branch = d_branch_ref[r, :, vs]
            factor = lax.rsqrt(jnp.mean(mixed * mixed, axis=1, keepdims=True) + EPS)
            normed = mixed * factor
            gate_logistic, gate_slope = slope(gate)
            d_scaled = d_branch * (gate * gate_logistic)
            d_gain_ref[...] += jnp.sum(d_scaled * normed, axis=0, keepdims=True)
            d_all_ref[r, :, chan + h * VALUE : chan + (h + 1) * VALUE] = (
                d_branch * normed * gain * gate_slope
            ).astype(LOW)
            d_normed = d_scaled * gain
            d_out = factor * (
                d_normed - normed * jnp.mean(d_normed * normed, axis=1, keepdims=True)
            )
            pair, beta, decay = f["pair"], f["beta_col"], f["decay_col"]
            inverse, updates, old = halves(inv_ref[0, at]), upd_ref[r, :, vs], state_ref[0, at]
            upd_parts, old_parts, out_parts = halves(updates), halves(old), halves(d_out)
            d_new = d_state[at]
            d_new_parts = halves(d_new)
            similar = product((keys,), (keys,), 1, 1)
            seen = product((query,), (keys,), 1, 1) * pair
            carried = product((keys,), d_new_parts)
            d_updates = product(halves(seen), out_parts, 0, 0) + f["last"] * carried
            d_targets = product(inverse, halves(d_updates), 0, 0)
            target_parts = halves(d_targets)
            below = jnp.where(row > col, -product(target_parts, upd_parts, 1, 1), 0.0)
            d_seen = product(out_parts, upd_parts, 1, 1)
            below_pair = below * pair
            d_similar = halves(below_pair * beta)
            d_seen_pair = halves(d_seen * pair)
            target_state = product(target_parts, old_parts, 1, 1)
            out_state = product(out_parts, old_parts, 1, 1)
            keys_wide, query_wide = keys.astype(F32), query.astype(F32)
            d_query = decay * out_state + product(d_seen_pair, (keys,))
            d_keys = (
                product(d_similar, (keys,))
                + product(d_similar, (keys,), 0, 0)
                + product(d_seen_pair, (query,), 0, 0)
                + f["last"] * product(upd_parts, d_new_parts, 1, 1)
                - (beta * decay) * target_state
            )
            d_values = beta * d_targets
            key_target = jnp.sum(keys_wide * target_state, axis=1, keepdims=True)
            by_beta = below_pair * similar
            d_beta = (
                jnp.sum(d_targets * values.astype(F32), axis=1, keepdims=True)
                - decay * key_target
                + jnp.sum(by_beta, axis=1, keepdims=True)
            )
            d_pair = by_beta * beta + d_seen * seen
            d_decay = jnp.sum(query_wide * out_state, axis=1, keepdims=True) - beta * key_target
            d_last = f["last"] * jnp.sum(updates * carried, axis=1, keepdims=True)
            at_last = jnp.sum(d_last, axis=0, keepdims=True) + f["decay_last"] * jnp.sum(
                jnp.sum(d_new * old, axis=1, keepdims=True), axis=0, keepdims=True
            )
            d_sums = (
                jnp.sum(d_pair, axis=1, keepdims=True)
                + decay * d_decay
                - d_last
                + jnp.where(position == BLOCK - 1, at_last, 0.0)
            )
            columns = jnp.where(lane == h, d_sums, columns)
            rows.append(jnp.sum(d_pair, axis=0, keepdims=True))
            d_betas.append(d_beta)
            d_state[at] = (
                f["decay_last"] * d_new
                + product((query,), halves(decay * d_out), 0, 0)
                - product((keys,), halves((beta * decay) * d_targets), 0, 0)
            )
            d_query = d_query.astype(LOW).astype(F32) * KEY ** (-0.5)
            d_keys = d_keys.astype(LOW).astype(F32)
            d_query_raw.append(
                query_factor
                * (d_query - query_unit * jnp.sum(d_query * query_unit, axis=1, keepdims=True))
            )
            d_key_raw.append(
                key_factor * (d_keys - key_unit * jnp.sum(d_keys * key_unit, axis=1, keepdims=True))
            )
            d_value_raw.append(d_values.astype(LOW).astype(F32))
        turned = jnp.concatenate(
            rows + [jnp.zeros((128 - heads, BLOCK), F32)], axis=0
        ).T
        upper = (row <= col).astype(LOW)
        d_aux = product((upper,), thirds(columns - turned))
        for h in range(heads):
            d_aux = jnp.where(lane == heads + h, d_betas[h], d_aux)
        d_rate = d_aux * factor_ref[r]
        d_all_ref[r, :, chan + hv :] = d_rate.astype(LOW)
        d_rate_ref[0:1, :] += jnp.sum(d_aux * aux, axis=0, keepdims=True)
        d_rate_ref[1:2, :] += jnp.sum(d_rate, axis=0, keepdims=True)
        d_conv = jnp.concatenate(d_query_raw + d_key_raw + d_value_raw, axis=1) * conv_slope
        d_ext_sum = taps[CONV - 1 : CONV, :] * d_conv
        d_taps_ref[CONV - 1 : CONV, :] += jnp.sum(d_conv * shifted(0), axis=0, keepdims=True)
        for lag in range(1, CONV):
            masked = d_conv * aux[:, 2 * heads + lag : 2 * heads + lag + 1]
            d_taps_ref[CONV - 1 - lag : CONV - lag, :] += jnp.sum(
                masked * shifted(lag), axis=0, keepdims=True
            )
            slot = r * (CONV - 1) + lag - 1
            d_ext[slot, :BLOCK, :] = masked
            d_ext_sum = (
                d_ext_sum + taps[CONV - 1 - lag : CONV - lag, :] * d_ext[slot, lag : lag + BLOCK, :]
            )
            d_ext[slot, BLOCK:, :] = d_ext[slot, :8, :]
        d_all_ref[r, :, :chan] = d_ext_sum.astype(LOW)


def mix_back(
    x, taps, aux, factor, gate, gain, mixed, inverses, updates, states, d_branch, heads
):
    length, chan = x.shape[1:]
    count = length // BLOCK
    hv = heads * VALUE
    here = lambda j: (0, count - 1 - j, 0)
    halo = lambda j: (0, jnp.maximum((count - 1 - j) * (BLOCK // 16) - 1, 0), 0)
    saved = lambda j: (count - 1 - j, 0, 0, 0)
    fixed = lambda j: (0, 0)
    return pl.pallas_call(
        functools.partial(mix_back_kernel, heads),
        grid=(count,),
        in_specs=[
            pl.BlockSpec((2, BLOCK, chan), here),
            pl.BlockSpec((2, 16, chan), halo),
            pl.BlockSpec((CONV, chan), fixed),
            pl.BlockSpec((2, BLOCK, 128), here),
            pl.BlockSpec((2, BLOCK, 128), here),
            pl.BlockSpec((2, BLOCK, hv), here),
            pl.BlockSpec((1, VALUE), fixed),
            pl.BlockSpec((2, BLOCK, hv), here),
            pl.BlockSpec((1, 2 * heads, BLOCK, BLOCK), saved),
            pl.BlockSpec((2, BLOCK, hv), here),
            pl.BlockSpec((1, 2 * heads, KEY, VALUE), saved),
            pl.BlockSpec((2, BLOCK, hv), here),
        ],
        out_specs=[
            pl.BlockSpec((2, BLOCK, chan + hv + 128), here),
            pl.BlockSpec((CONV, chan), fixed),
            pl.BlockSpec((1, VALUE), fixed),
            pl.BlockSpec((8, 128), fixed),
        ],
        out_shape=[
            jax.ShapeDtypeStruct((2, length, chan + hv + 128), LOW),
            jax.ShapeDtypeStruct((CONV, chan), F32),
            jax.ShapeDtypeStruct((1, VALUE), F32),
            jax.ShapeDtypeStruct((8, 128), F32),
        ],
        scratch_shapes=[
            pltpu.VMEM((2, BLOCK + 8, chan), F32),
            pltpu.VMEM((2 * (CONV - 1), BLOCK + 8, chan), F32),
            pltpu.VMEM((2 * heads, KEY, VALUE), F32),
        ],
        compiler_params=pltpu.CompilerParams(
            dimension_semantics=("arbitrary",), vmem_limit_bytes=48 * 1024 * 1024
        ),
        cost_estimate=pl.CostEstimate(
            flops=1_000_000, bytes_accessed=1_000_000, transcendentals=0
        ),
        name="mix_backward",
    )(x, x, taps, aux, factor, gate, gain, mixed, inverses, updates, states, d_branch)


def contract_rows(left, right):
    return lax.dot_general(
        left, right, (((1,), (1,)), ((), ())), preferred_element_type=jnp.float32
    )


def contract_tokens(left, right):
    return lax.dot_general(
        left, right, (((0,), (0,)), ((), ())), preferred_element_type=jnp.float32
    )


def silu_slope(value):
    logistic = jax.nn.sigmoid(value)
    return logistic * (1.0 + value * (1.0 - logistic))


def norm_back(normed, factor, grad):
    return factor * (grad - normed * jnp.mean(grad * normed, axis=-1, keepdims=True))


def swap_core(x):
    return lax.ppermute(x, "core", [(0, 1), (1, 0)])


def from_peer(x, axis, distance):
    return lax.ppermute(x, axis, [(i, i ^ distance) for i in range(lax.axis_size(axis))])


def plane_blocks(x):
    blocks = [x] + [from_peer(x, "seq", k) for k in range(1, lax.axis_size("seq"))]
    return blocks + [swap_core(b) for b in blocks]


def plane_gather(x):
    size, me = lax.axis_size("seq"), lax.axis_index("seq")
    tokens = x.shape[0]
    whole = jnp.zeros((2 * size * tokens,) + x.shape[1:], x.dtype)
    for k, block in enumerate(plane_blocks(x)):
        at = (k // size * size + (me ^ (k % size))) * tokens
        whole = lax.dynamic_update_slice(whole, block, (at, 0))
    return whole


def product_rows(left, right, first):
    half = left[0].shape[0] // 2
    at = slice(0, half) if first else slice(half, None)
    return sum(contract_rows(a[at], b) for a, b in zip(left, right))


def row_sum(left, right, far=None, kind=jnp.bfloat16):
    if far is None:
        far = product_rows(left, right, False).astype(kind)
    return product_rows(left, right, True) + swap_core(far).astype(jnp.float32)


def block_sum(row, ordered, kind=jnp.bfloat16):
    size, me = lax.axis_size("seq"), lax.axis_index("seq")
    tokens = row.shape[0] // size

    def block(k):
        at = (me ^ k) * tokens if ordered else k * tokens
        return lax.dynamic_slice_in_dim(row, at, tokens, 0)

    total = block(0)
    for k in range(1, size):
        total = total + from_peer(block(k).astype(kind), "seq", k).astype(jnp.float32)
    return total


def laid_out(x, axis):
    size, me = lax.axis_size(axis), lax.axis_index(axis)
    whole = jnp.zeros((size,) + x.shape, x.dtype)
    for k in range(size):
        block = from_peer(x, axis, k) if k else x
        whole = lax.dynamic_update_index_in_dim(whole, block, me ^ k, 0)
    return whole


def by_holder(parts, split):
    rows = parts[0].shape[0]
    return jnp.concatenate(
        [jnp.swapaxes(p.reshape(rows, split, -1), 0, 1) for p in parts], axis=2
    )


def plane_exchange(blocks):
    got = lax.all_to_all(blocks, PLANE, 0, 0)
    return got.reshape(-1, got.shape[2])


def along_z(x):
    return lax.all_gather(x, "z", axis=0, tiled=True)


def shard_sum(partial):
    return lax.psum_scatter(partial, "z", scatter_dimension=0, tiled=True)


def to_holders(mine, split):
    blocks = lax.all_to_all(mine.reshape(split, -1, mine.shape[1]), PLANE, 0, 0)
    return jnp.swapaxes(blocks, 0, 1).astype(jnp.float32)


def after(x, *done):
    return lax.optimization_barrier((x,) + done)[0]


def axis_sum(x, axis):
    blocks = [x] + [from_peer(x, axis, k) for k in range(1, lax.axis_size(axis))]
    while len(blocks) > 1:
        blocks = [p + q for p, q in zip(blocks[::2], blocks[1::2])]
    return blocks[0]


def all_sum(x):
    return axis_sum(axis_sum(axis_sum(x, "seq"), "core"), "z")


def on_device(
    hidden_in,
    boundary,
    norm_gain,
    proj_weight,
    rate_weight,
    conv_weight,
    log_rate,
    rate_bias,
    head_gain,
    out_weight,
    ffn_norm_gain,
    gate_up_weight,
    down_weight,
    grad_out,
):
    own = hidden_in.shape[1]
    width = hidden_in.shape[2]
    seq = lax.axis_size("seq")
    planes = lax.axis_size("z")
    split = 2 * seq
    length = own * seq
    tokens = 2 * length
    heads = HEADS // split
    hk, hv, ff = heads * KEY, heads * VALUE, FF // split
    chan = 2 * hk + hv
    me = lax.axis_index("seq")
    core = lax.axis_index("core")
    plane = lax.axis_index("z")
    here = core * seq + me
    rows = proj_weight.shape[0]

    def own_columns(whole, count):
        return lax.dynamic_slice_in_dim(whole, here * count, count, whole.ndim - 1)

    mix_in = by_holder(
        [
            proj_weight[:, :HK],
            proj_weight[:, HK : 2 * HK],
            proj_weight[:, 2 * HK : 2 * HK + HV],
        ],
        split,
    )
    others, hidden_in, mix_in = lax.optimization_barrier(
        ((proj_weight[:, 2 * HK + HV :], out_weight, gate_up_weight, down_weight), hidden_in, mix_in)
    )
    mix_in = lax.all_gather(mix_in, "z", axis=0)
    others = by_holder(
        [
            others[0],
            others[1],
            others[2][:, :FF],
            others[2][:, FF:],
            others[3],
            rate_weight[:, :HEADS],
            rate_weight[:, HEADS:],
        ],
        split,
    )
    x = hidden_in[0].astype(jnp.float32)
    scale = lax.rsqrt(jnp.mean(x * x, axis=1, keepdims=True) + EPS)
    normed = x * scale
    first_in = plane_gather((normed * norm_gain).astype(jnp.bfloat16))
    others = plane_exchange(after(others, first_in))
    at = 2 * hv + 3 * ff
    rate_rows = others[:, at : at + 2 * heads].T
    rate_in = jnp.zeros((2 * heads, width), jnp.bfloat16)
    for k in range(planes):
        block = from_peer(rate_rows, "z", k) if k else rate_rows
        rate_in = lax.dynamic_update_slice_in_dim(
            rate_in, block, (plane ^ k) * rows * split, 1
        )
    cut = ff * 3 // 4 // 128 * 128
    ffn = [
        jnp.concatenate([others[:, 2 * hv + i * ff : 2 * hv + (i + 1) * ff][:, p] for i in range(3)], axis=1)
        for p in (slice(0, cut), slice(cut, ff))
    ]
    mix_in = lax.all_to_all(jnp.swapaxes(mix_in, 0, 1), PLANE, 0, 0)
    mix_in = jnp.swapaxes(mix_in, 0, 1).reshape(width, chan)
    gate_out = along_z(others[:, : 2 * hv])
    gate_in, out_cols = gate_out[:, :hv], gate_out[:, hv:]

    bounds = jnp.concatenate([boundary, swap_core(boundary)], axis=0)
    positions = jnp.arange(length)
    start = jnp.logical_or(
        jnp.any(positions[None, :, None] == bounds[:, None, :], axis=2), positions == 0
    ).astype(jnp.float32)
    keep = jnp.ones((2, length), jnp.float32)
    keeps = []
    for lag in range(1, CONV):
        keep = keep * (1.0 - jnp.pad(start, ((0, 0), (lag - 1, 0)))[:, :length])
        keeps.append(keep)
    taps = jnp.concatenate(
        [
            own_columns(conv_weight[:, :HK], hk),
            own_columns(conv_weight[:, HK : 2 * HK], hk),
            own_columns(conv_weight[:, 2 * HK :], hv),
        ],
        axis=1,
    )
    own_rate, own_bias = own_columns(log_rate, heads), own_columns(rate_bias, heads)

    rates = contract_rows(first_in, rate_in)
    rates = rates.reshape(2, length, 2 * heads)
    rate_input = rates[:, :, :heads] + own_bias
    speed = -jnp.exp(own_rate)
    decay_log = speed * jax.nn.softplus(rate_input)
    beta = jax.nn.sigmoid(rates[:, :, heads:])
    aux = jnp.concatenate([decay_log, beta] + [s[:, :, None] for s in [start] + keeps], axis=2)
    aux = jnp.pad(aux, ((0, 0), (0, 0), (0, 128 - aux.shape[2])))
    factor = jnp.concatenate([speed * jax.nn.sigmoid(rate_input), beta * (1.0 - beta)], axis=2)
    factor = jnp.pad(factor, ((0, 0), (0, 0), (0, 128 - 2 * heads)))
    mix_in, aux, factor, grad_out = lax.optimization_barrier((mix_in, aux, factor, grad_out))
    cot = plane_blocks(grad_out[0])
    conv_in = jnp.dot(first_in, mix_in, preferred_element_type=jnp.float32)
    conv_in = conv_in.astype(jnp.bfloat16).reshape(2, length, chan)
    mixed, inverses, updates, states, final = mix(conv_in, taps, aux, heads)

    mixed, gate_in, ffn = lax.optimization_barrier((mixed, gate_in, ffn))
    ffn = [along_z(w) for w in ffn]
    gate = jnp.dot(first_in, gate_in, preferred_element_type=jnp.float32).reshape(2, length, hv)
    branch = []
    for h in range(heads):
        part = mixed[:, :, h * VALUE : (h + 1) * VALUE]
        norm = lax.rsqrt(jnp.mean(part * part, axis=2, keepdims=True) + EPS)
        branch.append(
            part * norm * head_gain * jax.nn.silu(gate[:, :, h * VALUE : (h + 1) * VALUE])
        )
    branch = jnp.concatenate(branch, axis=2).astype(jnp.bfloat16).reshape(tokens, hv)
    branch, cot = lax.optimization_barrier((branch, cot))
    cot = jnp.concatenate(cot, axis=0)
    hidden = x + block_sum(row_sum([branch], [out_cols], None, F32), True, F32)

    scale_two = lax.rsqrt(jnp.mean(hidden * hidden, axis=1, keepdims=True) + EPS)
    normed_two = hidden * scale_two
    second_in = jnp.concatenate(
        plane_blocks((normed_two * ffn_norm_gain).astype(jnp.bfloat16)), axis=0
    )
    inner, d_both = [], []
    grad_ffn = jnp.zeros((width, 3 * ff), jnp.bfloat16)
    for part in range(2):
        if part:
            grad_ffn, ffn[1] = lax.optimization_barrier((grad_ffn, ffn[1]))
        weight = ffn[part]
        units = weight.shape[1] // 3
        both_in, down_in = weight[:, : 2 * units], weight[:, 2 * units :]
        both = jnp.dot(second_in, both_in, preferred_element_type=jnp.float32)
        gate_part, up_part = both[:, :units], both[:, units:]
        gate_silu = jax.nn.silu(gate_part)
        inner.append((gate_silu * up_part).astype(jnp.bfloat16))
        d_inner = jnp.dot(cot, down_in, preferred_element_type=jnp.float32)
        d_both.append(
            jnp.concatenate(
                [d_inner * up_part * silu_slope(gate_part), d_inner * gate_silu], axis=1
            ).astype(jnp.bfloat16)
        )
        for at, grad in (
            (0, contract_tokens(second_in, d_both[-1])),
            (2 * units, contract_tokens(cot, inner[-1])),
        ):
            grad_ffn = lax.dynamic_update_slice(
                grad_ffn, grad.astype(jnp.bfloat16), (0, 3 * cut * part + at)
            )
    ups = [w[:, : 2 * w.shape[1] // 3] for w in ffn]
    downs = [w[:, 2 * w.shape[1] // 3 :] for w in ffn]
    d_both = after(d_both, grad_ffn)
    grad_ffn = shard_sum(grad_ffn)
    d_second = block_sum(row_sum(d_both, ups), False)
    grad_gain_two = jnp.sum(d_second * normed_two, axis=0)
    d_hidden = grad_out[0].astype(jnp.float32) + norm_back(
        normed_two, scale_two, d_second * ffn_norm_gain
    )

    d_mix = plane_gather(d_hidden.astype(jnp.bfloat16))
    d_branch = jnp.dot(d_mix, out_cols, preferred_element_type=jnp.float32)
    fed = product_rows(inner, downs, False).astype(jnp.bfloat16)
    d_branch, fed, final = lax.optimization_barrier((d_branch, fed, final))
    result = hidden + block_sum(row_sum(inner, downs, fed), False)
    result = result.astype(jnp.bfloat16)
    final = final.reshape(2, heads, VALUE, KEY).astype(jnp.bfloat16)
    other = swap_core(final[1])
    pair = jnp.zeros((2, heads, VALUE, KEY), jnp.bfloat16)
    pair = lax.dynamic_update_index_in_dim(pair, final[0], core, 0)
    pair = lax.dynamic_update_index_in_dim(pair, other, 1 - core, 0)
    final_state = jnp.swapaxes(laid_out(pair, "seq"), 0, 1).astype(jnp.float32)
    final_state = final_state.reshape(1, HEADS, VALUE, KEY)

    d_all, grad_taps, grad_head_gain, rate_sums = mix_back(
        conv_in,
        taps,
        aux,
        factor,
        gate,
        head_gain[None],
        mixed,
        inverses,
        updates,
        states,
        d_branch.reshape(2, length, hv),
        heads,
    )
    d_all = d_all.reshape(tokens, chan + hv + 128)
    whole_in = jnp.concatenate(
        [mix_in, gate_in, jnp.pad(rate_in.T, ((0, 0), (0, 128 - 2 * heads)))], axis=1
    )
    row_first = row_sum([d_all], [whole_in])
    grad_proj = contract_tokens(first_in, d_all[:, : chan + hv]).astype(jnp.bfloat16)
    grad_proj = jnp.concatenate(
        [grad_proj, contract_tokens(d_mix, branch).astype(jnp.bfloat16)], axis=1
    )
    grad_proj, grad_ffn, row_first = lax.optimization_barrier((grad_proj, grad_ffn, row_first))
    d_first = block_sum(row_first, True)
    grad_proj = shard_sum(grad_proj)
    grad_ffn = to_holders(grad_ffn, split)
    def hidden_columns(at):
        first, second = grad_ffn[:, :, : 3 * cut], grad_ffn[:, :, 3 * cut :]
        return jnp.concatenate(
            [g[:, :, at * u : (at + 1) * u] for g, u in ((first, cut), (second, ff - cut))], axis=2
        ).reshape(rows, FF)

    grad_gate_up = jnp.concatenate([hidden_columns(0), hidden_columns(1)], axis=1)
    grad_down = hidden_columns(2)

    grad_rate = lax.dot_general(
        d_all[:, chan + hv :], first_in, (((0,), (0,)), ((), ())), preferred_element_type=jnp.float32
    )[: 2 * heads]
    small = jnp.concatenate(
        [
            grad_taps,
            grad_rate.reshape(-1, chan),
            jnp.pad(rate_sums[:2].reshape(1, -1), ((0, 0), (0, chan - 256))),
        ],
        axis=0,
    )
    small = laid_out(laid_out(axis_sum(small, "z"), "seq"), "core")
    small = small.reshape((split,) + small.shape[2:])
    grad_conv = jnp.swapaxes(small[:, :CONV], 0, 1)
    grad_conv = jnp.concatenate(
        [
            grad_conv[:, :, :hk].reshape(CONV, HK),
            grad_conv[:, :, hk : 2 * hk].reshape(CONV, HK),
            grad_conv[:, :, 2 * hk :].reshape(CONV, HV),
        ],
        axis=1,
    )
    rate_sums = small[:, -1, :256].reshape(split, 2, 128)
    grad_rate = small[:, CONV:-1].reshape(split, 2, heads, width)
    grad_rate = jnp.swapaxes(grad_rate, 0, 1).reshape(2 * HEADS, width)
    grad_rate = lax.dynamic_slice_in_dim(grad_rate, (plane * split + here) * rows, rows, 1).T

    d_first, result, final_state = lax.optimization_barrier((d_first, result, final_state))
    grad_gain_one = jnp.sum(d_first * normed, axis=0)
    sums = all_sum(jnp.concatenate([grad_gain_one, grad_gain_two, grad_head_gain[0]]))
    d_row = d_hidden + norm_back(normed, scale, d_first * norm_gain)
    d_row = d_row.astype(jnp.bfloat16)
    holders_proj = to_holders(grad_proj, split)
    grad_proj = jnp.concatenate(
        [
            holders_proj[:, :, :hk].reshape(rows, HK),
            holders_proj[:, :, hk : 2 * hk].reshape(rows, HK),
            holders_proj[:, :, 2 * hk : chan].reshape(rows, HV),
            holders_proj[:, :, chan : chan + hv].reshape(rows, HV),
        ],
        axis=1,
    )
    return (
        result[None],
        d_row[None],
        final_state,
        sums[:width],
        grad_proj,
        grad_rate,
        grad_conv,
        rate_sums[:, 0, :heads].reshape(HEADS),
        rate_sums[:, 1, :heads].reshape(HEADS),
        sums[2 * width :],
        holders_proj[:, :, chan + hv :].reshape(rows, HV),
        sums[width : 2 * width],
        grad_gate_up,
        grad_down,
    )


def solution(mesh):
    dp, seq = mesh.shape["dp"], mesh.shape["seq"]
    planes = Mesh(mesh.devices.reshape(dp // 2, 2, seq), ("z", "core", "seq"))
    row = ("z", "core")
    every = ("z", "core", "seq")
    in_specs = (
        P(row, "seq", None),
        P(row, None),
        P(),
        P(every, None),
        P(every, None),
        P(),
        P(),
        P(),
        P(),
        P(every, None),
        P(),
        P(every, None),
        P(every, None),
        P(row, "seq", None),
    )
    out_specs = (
        P(row, "seq", None),
        P(row, "seq", None),
        P(row, None, None, None),
        P(),
        P(every, None),
        P(every, None),
        P(),
        P(),
        P(),
        P(),
        P(every, None),
        P(),
        P(every, None),
        P(every, None),
    )
    return jax.shard_map(
        on_device, mesh=planes, in_specs=in_specs, out_specs=out_specs, check_vma=False
    )
```

```python
import functools

import jax
import jax.numpy as jnp
from jax import lax
from jax.experimental import pallas as pl
from jax.experimental.pallas import tpu as pltpu
from jax.sharding import Mesh
from jax.sharding import PartitionSpec as P

HEADS = 16
FF = 5504
HK = 2048
HV = 4096
PLANE = ("core", "seq")
KEY = 128
VALUE = 256
CONV = 4
EPS = 1e-06
BLOCK = 128
F32 = jnp.float32
LOW = jnp.bfloat16


def halves(x):
    high = x.astype(LOW)
    return (high, (x - high.astype(F32)).astype(LOW))


def thirds(x):
    high = x.astype(LOW)
    rest = x - high.astype(F32)
    middle = rest.astype(LOW)
    return (high, middle, (rest - middle.astype(F32)).astype(LOW))


def product(left, right, left_dim=1, right_dim=0):
    total = None
    for i, a in enumerate(left):
        for j, b in enumerate(right):
            if i + j < max(len(left), len(right)):
                term = lax.dot_general(
                    a, b, (((left_dim,), (right_dim,)), ((), ())), preferred_element_type=F32
                )
                total = term if total is None else total + term
    return total


def places():
    row = lax.broadcasted_iota(jnp.int32, (BLOCK, BLOCK), 0)
    col = lax.broadcasted_iota(jnp.int32, (BLOCK, BLOCK), 1)
    return row, col


def running(aux, row, col):
    lower = (row >= col).astype(LOW)
    return product((lower,), thirds(aux))


def solved(negated, row, col):
    same = (row >> 4) == (col >> 4)
    power = [jnp.where(same, n, 0.0) for n in negated]
    inverse = [(row == col).astype(F32) + p for p in power]
    for _ in range(3):
        parts = [halves(p) for p in power]
        power = [product(p, p) for p in parts]
        parts = [(halves(i), halves(p)) for i, p in zip(inverse, power)]
        inverse = [i + product(*p) for i, p in zip(inverse, parts)]
    for bits in (4, 5, 6):
        beside = jnp.logical_and(
            (row >> (bits + 1)) == (col >> (bits + 1)), (row >> bits) != (col >> bits)
        )
        off = [halves(jnp.where(beside, n, 0.0)) for n in negated]
        parts = [halves(i) for i in inverse]
        off = [halves(product(o, p)) for o, p in zip(off, parts)]
        inverse = [i + product(p, o) for i, p, o in zip(inverse, parts, off)]
    return inverse


def decays(aux, row, col, heads):
    sums = running(aux, row, col)
    turned = sums.T
    aux_turned = aux.T
    seg_col, seg_row = sums[:, 2 * heads : 2 * heads + 1], turned[2 * heads : 2 * heads + 1, :]
    joined = jnp.logical_and(row >= col, seg_col == seg_row)
    seg_last = sums[BLOCK - 1 :, 2 * heads : 2 * heads + 1]
    out = []
    for h in range(heads):
        g_col, g_row = sums[:, h : h + 1], turned[h : h + 1, :]
        pair = jnp.where(joined, jnp.exp(jnp.where(joined, g_col - g_row, 0.0)), 0.0)
        alive_col = jnp.where(seg_col == 0.0, jnp.exp(g_col), 0.0)
        alive_row = jnp.where(seg_row == 0.0, jnp.exp(g_row), 0.0)
        last = jnp.where(seg_col == seg_last, jnp.exp(sums[BLOCK - 1 :, h : h + 1] - g_col), 0.0)
        out.append(
            dict(
                pair=pair,
                decay_col=alive_col,
                decay_row=alive_row,
                decay_last=alive_col[BLOCK - 1 :, :],
                last=last,
                beta_col=aux[:, heads + h : heads + h + 1],
                beta_row=aux_turned[heads + h : heads + h + 1, :],
            )
        )
    return out


def convolved(ext, taps, aux, heads):
    total = taps[CONV - 1 : CONV, :] * ext(0)
    for lag in range(1, CONV):
        keep = aux[:, 2 * heads + lag : 2 * heads + lag + 1]
        total = total + taps[CONV - 1 - lag : CONV - lag, :] * (ext(lag) * keep)
    return total


def unit(raw):
    factor = lax.rsqrt(jnp.sum(raw * raw, axis=1, keepdims=True) + EPS)
    return raw * factor, factor


def mix_kernel(
    heads, x_ref, taps_ref, aux_ref, mixed_ref, inv_ref, upd_ref, state_ref, final_ref, ext, state
):
    step = pl.program_id(0)
    hk = heads * KEY
    row, col = places()

    @pl.when(step == 0)
    def _():
        state[...] = jnp.zeros_like(state)
        ext[:, :8, :] = jnp.zeros_like(ext[:, :8, :])

    state_ref[0] = state[...]
    taps = taps_ref[...]
    facts, query, keys, values, spans = [], [], [], [], []
    for r in range(2):
        aux = aux_ref[r]
        ext[r, 8:, :] = x_ref[r].astype(F32)
        conv = convolved(lambda lag: ext[r, 8 - lag : 8 - lag + BLOCK, :], taps, aux, heads)
        act = conv * jax.nn.sigmoid(conv)
        ext[r, :8, :] = ext[r, BLOCK:, :]
        facts += decays(aux, row, col, heads)
        for h in range(heads):
            spans.append((r, slice(h * VALUE, (h + 1) * VALUE)))
            query.append(
                (unit(act[:, h * KEY : (h + 1) * KEY])[0] * KEY ** (-0.5)).astype(LOW)
            )
            keys.append(unit(act[:, hk + h * KEY : hk + (h + 1) * KEY])[0].astype(LOW))
            values.append(act[:, 2 * hk + h * VALUE : 2 * hk + (h + 1) * VALUE].astype(LOW))
    every = range(2 * heads)
    similar = [product((k,), (k,), 1, 1) for k in keys]
    inverse = solved(
        [
            jnp.where(row > col, -(f["beta_col"] * f["pair"] * s), 0.0)
            for f, s in zip(facts, similar)
        ],
        row,
        col,
    )
    seen = [product((q,), (k,), 1, 1) * f["pair"] for q, k, f in zip(query, keys, facts)]
    old = [state[at] for at in every]
    old_parts = [halves(o) for o in old]
    asked = [product((q,), o) for q, o in zip(query, old_parts)]
    scaled = [i * f["beta_row"] for i, f in zip(inverse, facts)]
    weights = [
        halves(product(halves(s * f["decay_row"]), (k,))) for s, f, k in zip(scaled, facts, keys)
    ]
    updates = [product(halves(s), (v,)) for s, v in zip(scaled, values)]
    updates = [u - product(w, o) for u, w, o in zip(updates, weights, old_parts)]
    for at in every:
        f, (r, vs) = facts[at], spans[at]
        inv_ref[0, at] = inverse[at]
        upd_ref[r, :, vs] = updates[at]
        state[at] = f["decay_last"] * old[at] + product(
            (keys[at],), halves(f["last"] * updates[at]), 0, 0
        )
    for at in every:
        r, vs = spans[at]
        mixed_ref[r, :, vs] = facts[at]["decay_col"] * asked[at] + product(
            halves(seen[at]), halves(updates[at])
        )

    @pl.when(step == pl.num_programs(0) - 1)
    def _():
        for at in range(2 * heads):
            final_ref[at] = state[at].T


def mix(x, taps, aux, heads):
    length, chan = x.shape[1:]
    count = length // BLOCK
    hv = heads * VALUE
    here = lambda j: (0, j, 0)
    saved = lambda j: (j, 0, 0, 0)
    return pl.pallas_call(
        functools.partial(mix_kernel, heads),
        grid=(count,),
        in_specs=[
            pl.BlockSpec((2, BLOCK, chan), here),
            pl.BlockSpec((CONV, chan), lambda j: (0, 0)),
            pl.BlockSpec((2, BLOCK, 128), here),
        ],
        out_specs=[
            pl.BlockSpec((2, BLOCK, hv), here),
            pl.BlockSpec((1, 2 * heads, BLOCK, BLOCK), saved),
            pl.BlockSpec((2, BLOCK, hv), here),
            pl.BlockSpec((1, 2 * heads, KEY, VALUE), saved),
            pl.BlockSpec((2 * heads, VALUE, KEY), lambda j: (0, 0, 0)),
        ],
        out_shape=[
            jax.ShapeDtypeStruct((2, length, hv), F32),
            jax.ShapeDtypeStruct((count, 2 * heads, BLOCK, BLOCK), F32),
            jax.ShapeDtypeStruct((2, length, hv), F32),
            jax.ShapeDtypeStruct((count, 2 * heads, KEY, VALUE), F32),
            jax.ShapeDtypeStruct((2 * heads, VALUE, KEY), F32),
        ],
        scratch_shapes=[
            pltpu.VMEM((2, BLOCK + 8, chan), F32),
            pltpu.VMEM((2 * heads, KEY, VALUE), F32),
        ],
        compiler_params=pltpu.CompilerParams(
            dimension_semantics=("arbitrary",), vmem_limit_bytes=48 * 1024 * 1024
        ),
        cost_estimate=pl.CostEstimate(
            flops=1_000_000, bytes_accessed=1_000_000, transcendentals=0
        ),
        name="mix_forward",
    )(x, taps, aux)


def slope(value):
    logistic = jax.nn.sigmoid(value)
    return logistic, logistic * (1.0 + value * (1.0 - logistic))


def mix_back_kernel(
    heads,
    x_ref,
    halo_ref,
    taps_ref,
    aux_ref,
    factor_ref,
    gate_ref,
    gain_ref,
    mixed_ref,
    inv_ref,
    upd_ref,
    state_ref,
    d_branch_ref,
    d_all_ref,
    d_taps_ref,
    d_gain_ref,
    d_rate_ref,
    ext,
    d_ext,
    d_state,
):
    step = pl.program_id(0)
    first_block = step == pl.num_programs(0) - 1
    hk, hv = heads * KEY, heads * VALUE
    chan = 2 * hk + hv
    row, col = places()
    lane = lax.broadcasted_iota(jnp.int32, (BLOCK, 128), 1)
    position = lax.broadcasted_iota(jnp.int32, (BLOCK, 1), 0)

    @pl.when(step == 0)
    def _():
        d_state[...] = jnp.zeros_like(d_state)
        d_ext[:, BLOCK:, :] = jnp.zeros_like(d_ext[:, BLOCK:, :])
        d_taps_ref[...] = jnp.zeros_like(d_taps_ref)
        d_gain_ref[...] = jnp.zeros_like(d_gain_ref)
        d_rate_ref[...] = jnp.zeros_like(d_rate_ref)

    taps = taps_ref[...]
    gain = gain_ref[...]
    conv_slope, facts, spans = [], [], []
    query_unit, query_factor, key_unit, key_factor, values = [], [], [], [], []
    for r in range(2):
        aux = aux_ref[r]
        before = halo_ref[r].astype(F32)[8:, :]
        ext[r, :8, :] = jnp.where(first_block, 0.0, before)
        ext[r, 8:, :] = x_ref[r].astype(F32)
        conv = convolved(lambda lag: ext[r, 8 - lag : 8 - lag + BLOCK, :], taps, aux, heads)
        logistic, conv_grad = slope(conv)
        conv_slope.append(conv_grad)
        act = conv * logistic
        facts += decays(aux, row, col, heads)
        for h in range(heads):
            spans.append((r, slice(h * VALUE, (h + 1) * VALUE)))
            normal, factor = unit(act[:, h * KEY : (h + 1) * KEY])
            query_unit.append(normal)
            query_factor.append(factor)
            normal, factor = unit(act[:, hk + h * KEY : hk + (h + 1) * KEY])
            key_unit.append(normal)
            key_factor.append(factor)
            values.append(act[:, 2 * hk + h * VALUE : 2 * hk + (h + 1) * VALUE].astype(LOW))
    every = range(2 * heads)
    query = [(q * KEY ** (-0.5)).astype(LOW) for q in query_unit]
    keys = [k.astype(LOW) for k in key_unit]

    d_out = []
    for r, vs in spans:
        mixed = mixed_ref[r, :, vs]
        gate = gate_ref[r, :, vs]
        d_branch = d_branch_ref[r, :, vs]
        factor = lax.rsqrt(jnp.mean(mixed * mixed, axis=1, keepdims=True) + EPS)
        normed = mixed * factor
        gate_logistic, gate_slope = slope(gate)
        d_scaled = d_branch * (gate * gate_logistic)
        d_gain_ref[...] += jnp.sum(d_scaled * normed, axis=0, keepdims=True)
        d_all_ref[r, :, chan + vs.start : chan + vs.stop] = (
            d_branch * normed * gain * gate_slope
        ).astype(LOW)
        d_normed = d_scaled * gain
        d_out.append(
            factor * (d_normed - normed * jnp.mean(d_normed * normed, axis=1, keepdims=True))
        )

    pair = [f["pair"] for f in facts]
    beta = [f["beta_col"] for f in facts]
    decay = [f["decay_col"] for f in facts]
    last = [f["last"] for f in facts]
    inverse = [halves(inv_ref[0, at]) for at in every]
    old = [state_ref[0, at] for at in every]
    d_new = [d_state[at] for at in every]
    out_parts = [halves(d) for d in d_out]
    d_new_parts = [halves(d) for d in d_new]
    seen = [product((q,), (k,), 1, 1) * p for q, k, p in zip(query, keys, pair)]
    carried = [product((k,), d) for k, d in zip(keys, d_new_parts)]
    d_updates = [
        product(halves(s), o, 0, 0) + t * c
        for s, o, t, c in zip(seen, out_parts, last, carried)
    ]
    d_targets = [product(i, halves(d), 0, 0) for i, d in zip(inverse, d_updates)]
    for at in every:
        d_state[at] = (
            facts[at]["decay_last"] * d_new[at]
            + product((query[at],), halves(decay[at] * d_out[at]), 0, 0)
            - product((keys[at],), halves((beta[at] * decay[at]) * d_targets[at]), 0, 0)
        )

    updates = [upd_ref[r, :, vs] for r, vs in spans]
    upd_parts = [halves(u) for u in updates]
    old_parts = [halves(o) for o in old]
    target_parts = [halves(d) for d in d_targets]
    similar = [product((k,), (k,), 1, 1) for k in keys]
    below_pair = [
        jnp.where(row > col, -product(t, u, 1, 1), 0.0) * p
        for t, u, p in zip(target_parts, upd_parts, pair)
    ]
    d_seen = [product(o, u, 1, 1) for o, u in zip(out_parts, upd_parts)]
    target_state = [product(t, o, 1, 1) for t, o in zip(target_parts, old_parts)]
    out_state = [product(d, o, 1, 1) for d, o in zip(out_parts, old_parts)]
    d_similar = [halves(b * t) for b, t in zip(below_pair, beta)]
    d_seen_pair = [halves(d * p) for d, p in zip(d_seen, pair)]
    d_query = [
        d * o + product(s, (k,)) for d, o, s, k in zip(decay, out_state, d_seen_pair, keys)
    ]
    d_keys = [
        product(d_similar[at], (keys[at],))
        + product(d_similar[at], (keys[at],), 0, 0)
        + product(d_seen_pair[at], (query[at],), 0, 0)
        + last[at] * product(upd_parts[at], d_new_parts[at], 1, 1)
        - (beta[at] * decay[at]) * target_state[at]
        for at in every
    ]

    for r in range(2):
        aux = aux_ref[r]
        columns = jnp.zeros((BLOCK, 128), F32)
        rows, d_betas = [], []
        d_query_raw, d_key_raw, d_value_raw = [], [], []
        for h in range(heads):
            at = r * heads + h
            key_target = jnp.sum(keys[at].astype(F32) * target_state[at], axis=1, keepdims=True)
            by_beta = below_pair[at] * similar[at]
            d_betas.append(
                jnp.sum(d_targets[at] * values[at].astype(F32), axis=1, keepdims=True)
                - decay[at] * key_target
                + jnp.sum(by_beta, axis=1, keepdims=True)
            )
            d_pair = by_beta * beta[at] + d_seen[at] * seen[at]
            d_decay = (
                jnp.sum(query[at].astype(F32) * out_state[at], axis=1, keepdims=True)
                - beta[at] * key_target
            )
            d_last = last[at] * jnp.sum(updates[at] * carried[at], axis=1, keepdims=True)
            at_last = jnp.sum(d_last, axis=0, keepdims=True) + facts[at]["decay_last"] * jnp.sum(
                jnp.sum(d_new[at] * old[at], axis=1, keepdims=True), axis=0, keepdims=True
            )
            d_sums = (
                jnp.sum(d_pair, axis=1, keepdims=True)
                + decay[at] * d_decay
                - d_last
                + jnp.where(position == BLOCK - 1, at_last, 0.0)
            )
            columns = jnp.where(lane == h, d_sums, columns)
            rows.append(jnp.sum(d_pair, axis=0, keepdims=True))
            d_unit = d_query[at].astype(LOW).astype(F32) * KEY ** (-0.5)
            d_query_raw.append(
                query_factor[at]
                * (d_unit - query_unit[at] * jnp.sum(d_unit * query_unit[at], axis=1, keepdims=True))
            )
            d_unit = d_keys[at].astype(LOW).astype(F32)
            d_key_raw.append(
                key_factor[at]
                * (d_unit - key_unit[at] * jnp.sum(d_unit * key_unit[at], axis=1, keepdims=True))
            )
            d_value_raw.append((beta[at] * d_targets[at]).astype(LOW).astype(F32))
        turned = jnp.concatenate(rows + [jnp.zeros((128 - heads, BLOCK), F32)], axis=0).T
        upper = (row <= col).astype(LOW)
        d_aux = product((upper,), thirds(columns - turned))
        for h in range(heads):
            d_aux = jnp.where(lane == heads + h, d_betas[h], d_aux)
        d_rate = d_aux * factor_ref[r]
        d_all_ref[r, :, chan + hv :] = d_rate.astype(LOW)
        d_rate_ref[0:1, :] += jnp.sum(d_aux * aux, axis=0, keepdims=True)
        d_rate_ref[1:2, :] += jnp.sum(d_rate, axis=0, keepdims=True)
        d_conv = jnp.concatenate(d_query_raw + d_key_raw + d_value_raw, axis=1) * conv_slope[r]
        d_ext_sum = taps[CONV - 1 : CONV, :] * d_conv
        d_taps_ref[CONV - 1 : CONV, :] += jnp.sum(d_conv * ext[r, 8:, :], axis=0, keepdims=True)
        for lag in range(1, CONV):
            masked = d_conv * aux[:, 2 * heads + lag : 2 * heads + lag + 1]
            d_taps_ref[CONV - 1 - lag : CONV - lag, :] += jnp.sum(
                masked * ext[r, 8 - lag : 8 - lag + BLOCK, :], axis=0, keepdims=True
            )
            slot = r * (CONV - 1) + lag - 1
            d_ext[slot, :BLOCK, :] = masked
            d_ext_sum = (
                d_ext_sum + taps[CONV - 1 - lag : CONV - lag, :] * d_ext[slot, lag : lag + BLOCK, :]
            )
            d_ext[slot, BLOCK:, :] = d_ext[slot, :8, :]
        d_all_ref[r, :, :chan] = d_ext_sum.astype(LOW)


def mix_back(
    x, taps, aux, factor, gate, gain, mixed, inverses, updates, states, d_branch, heads
):
    length, chan = x.shape[1:]
    count = length // BLOCK
    hv = heads * VALUE
    here = lambda j: (0, count - 1 - j, 0)
    halo = lambda j: (0, jnp.maximum((count - 1 - j) * (BLOCK // 16) - 1, 0), 0)
    saved = lambda j: (count - 1 - j, 0, 0, 0)
    fixed = lambda j: (0, 0)
    return pl.pallas_call(
        functools.partial(mix_back_kernel, heads),
        grid=(count,),
        in_specs=[
            pl.BlockSpec((2, BLOCK, chan), here),
            pl.BlockSpec((2, 16, chan), halo),
            pl.BlockSpec((CONV, chan), fixed),
            pl.BlockSpec((2, BLOCK, 128), here),
            pl.BlockSpec((2, BLOCK, 128), here),
            pl.BlockSpec((2, BLOCK, hv), here),
            pl.BlockSpec((1, VALUE), fixed),
            pl.BlockSpec((2, BLOCK, hv), here),
            pl.BlockSpec((1, 2 * heads, BLOCK, BLOCK), saved),
            pl.BlockSpec((2, BLOCK, hv), here),
            pl.BlockSpec((1, 2 * heads, KEY, VALUE), saved),
            pl.BlockSpec((2, BLOCK, hv), here),
        ],
        out_specs=[
            pl.BlockSpec((2, BLOCK, chan + hv + 128), here),
            pl.BlockSpec((CONV, chan), fixed),
            pl.BlockSpec((1, VALUE), fixed),
            pl.BlockSpec((8, 128), fixed),
        ],
        out_shape=[
            jax.ShapeDtypeStruct((2, length, chan + hv + 128), LOW),
            jax.ShapeDtypeStruct((CONV, chan), F32),
            jax.ShapeDtypeStruct((1, VALUE), F32),
            jax.ShapeDtypeStruct((8, 128), F32),
        ],
        scratch_shapes=[
            pltpu.VMEM((2, BLOCK + 8, chan), F32),
            pltpu.VMEM((2 * (CONV - 1), BLOCK + 8, chan), F32),
            pltpu.VMEM((2 * heads, KEY, VALUE), F32),
        ],
        compiler_params=pltpu.CompilerParams(
            dimension_semantics=("arbitrary",), vmem_limit_bytes=48 * 1024 * 1024
        ),
        cost_estimate=pl.CostEstimate(
            flops=1_000_000, bytes_accessed=1_000_000, transcendentals=0
        ),
        name="mix_backward",
    )(x, x, taps, aux, factor, gate, gain, mixed, inverses, updates, states, d_branch)


def contract_rows(left, right):
    return lax.dot_general(
        left, right, (((1,), (1,)), ((), ())), preferred_element_type=jnp.float32
    )


def contract_tokens(left, right):
    return lax.dot_general(
        left, right, (((0,), (0,)), ((), ())), preferred_element_type=jnp.float32
    )


def silu_slope(value):
    logistic = jax.nn.sigmoid(value)
    return logistic * (1.0 + value * (1.0 - logistic))


def norm_back(normed, factor, grad):
    return factor * (grad - normed * jnp.mean(grad * normed, axis=-1, keepdims=True))


def swap_core(x):
    return lax.ppermute(x, "core", [(0, 1), (1, 0)])


def from_peer(x, axis, distance):
    return lax.ppermute(x, axis, [(i, i ^ distance) for i in range(lax.axis_size(axis))])


def plane_blocks(x):
    blocks = [x] + [from_peer(x, "seq", k) for k in range(1, lax.axis_size("seq"))]
    return blocks + [swap_core(b) for b in blocks]


def plane_gather(x):
    size, me = lax.axis_size("seq"), lax.axis_index("seq")
    tokens = x.shape[0]
    whole = jnp.zeros((2 * size * tokens,) + x.shape[1:], x.dtype)
    for k, block in enumerate(plane_blocks(x)):
        at = (k // size * size + (me ^ (k % size))) * tokens
        whole = lax.dynamic_update_slice(whole, block, (at, 0))
    return whole


def product_rows(left, right, first):
    half = left[0].shape[0] // 2
    at = slice(0, half) if first else slice(half, None)
    return sum(contract_rows(a[at], b) for a, b in zip(left, right))


def row_sum(left, right, far=None, kind=jnp.bfloat16):
    if far is None:
        far = product_rows(left, right, False).astype(kind)
    return product_rows(left, right, True) + swap_core(far).astype(jnp.float32)


def block_sum(row, ordered, kind=jnp.bfloat16):
    size, me = lax.axis_size("seq"), lax.axis_index("seq")
    tokens = row.shape[0] // size

    def block(k):
        at = (me ^ k) * tokens if ordered else k * tokens
        return lax.dynamic_slice_in_dim(row, at, tokens, 0)

    total = block(0)
    for k in range(1, size):
        total = total + from_peer(block(k).astype(kind), "seq", k).astype(jnp.float32)
    return total


def laid_out(x, axis):
    size, me = lax.axis_size(axis), lax.axis_index(axis)
    whole = jnp.zeros((size,) + x.shape, x.dtype)
    for k in range(size):
        block = from_peer(x, axis, k) if k else x
        whole = lax.dynamic_update_index_in_dim(whole, block, me ^ k, 0)
    return whole


def by_holder(parts, split):
    rows = parts[0].shape[0]
    return jnp.concatenate(
        [jnp.swapaxes(p.reshape(rows, split, -1), 0, 1) for p in parts], axis=2
    )


def plane_exchange(blocks):
    got = lax.all_to_all(blocks, PLANE, 0, 0)
    return got.reshape(-1, got.shape[2])


def along_z(x):
    return lax.all_gather(x, "z", axis=0, tiled=True)


def shard_sum(partial):
    return lax.psum_scatter(partial, "z", scatter_dimension=0, tiled=True)


def to_holders(mine, split):
    blocks = lax.all_to_all(mine.reshape(split, -1, mine.shape[1]), PLANE, 0, 0)
    return jnp.swapaxes(blocks, 0, 1).astype(jnp.float32)


def after(x, *done):
    return lax.optimization_barrier((x,) + done)[0]


def axis_sum(x, axis):
    blocks = [x] + [from_peer(x, axis, k) for k in range(1, lax.axis_size(axis))]
    while len(blocks) > 1:
        blocks = [p + q for p, q in zip(blocks[::2], blocks[1::2])]
    return blocks[0]


def all_sum(x):
    return axis_sum(axis_sum(axis_sum(x, "seq"), "core"), "z")


def on_device(
    hidden_in,
    boundary,
    norm_gain,
    proj_weight,
    rate_weight,
    conv_weight,
    log_rate,
    rate_bias,
    head_gain,
    out_weight,
    ffn_norm_gain,
    gate_up_weight,
    down_weight,
    grad_out,
):
    own = hidden_in.shape[1]
    width = hidden_in.shape[2]
    seq = lax.axis_size("seq")
    planes = lax.axis_size("z")
    split = 2 * seq
    length = own * seq
    tokens = 2 * length
    heads = HEADS // split
    hk, hv, ff = heads * KEY, heads * VALUE, FF // split
    chan = 2 * hk + hv
    me = lax.axis_index("seq")
    core = lax.axis_index("core")
    plane = lax.axis_index("z")
    here = core * seq + me
    rows = proj_weight.shape[0]

    def own_columns(whole, count):
        return lax.dynamic_slice_in_dim(whole, here * count, count, whole.ndim - 1)

    mix_in = by_holder(
        [
            proj_weight[:, :HK],
            proj_weight[:, HK : 2 * HK],
            proj_weight[:, 2 * HK : 2 * HK + HV],
        ],
        split,
    )
    others, hidden_in, mix_in = lax.optimization_barrier(
        ((proj_weight[:, 2 * HK + HV :], out_weight, gate_up_weight, down_weight), hidden_in, mix_in)
    )
    mix_in = lax.all_gather(mix_in, "z", axis=0)
    others = by_holder(
        [
            others[0],
            others[1],
            others[2][:, :FF],
            others[2][:, FF:],
            others[3],
            rate_weight[:, :HEADS],
            rate_weight[:, HEADS:],
        ],
        split,
    )
    x = hidden_in[0].astype(jnp.float32)
    scale = lax.rsqrt(jnp.mean(x * x, axis=1, keepdims=True) + EPS)
    normed = x * scale
    first_in = plane_gather((normed * norm_gain).astype(jnp.bfloat16))
    others = plane_exchange(after(others, first_in))
    at = 2 * hv + 3 * ff
    rate_rows = others[:, at : at + 2 * heads].T
    rate_in = jnp.zeros((2 * heads, width), jnp.bfloat16)
    for k in range(planes):
        block = from_peer(rate_rows, "z", k) if k else rate_rows
        rate_in = lax.dynamic_update_slice_in_dim(
            rate_in, block, (plane ^ k) * rows * split, 1
        )
    cut = ff * 3 // 4 // 128 * 128
    ffn = [
        jnp.concatenate([others[:, 2 * hv + i * ff : 2 * hv + (i + 1) * ff][:, p] for i in range(3)], axis=1)
        for p in (slice(0, cut), slice(cut, ff))
    ]
    mix_in = lax.all_to_all(jnp.swapaxes(mix_in, 0, 1), PLANE, 0, 0)
    mix_in = jnp.swapaxes(mix_in, 0, 1).reshape(width, chan)
    gate_out = along_z(others[:, : 2 * hv])
    gate_in, out_cols = gate_out[:, :hv], gate_out[:, hv:]

    bounds = jnp.concatenate([boundary, swap_core(boundary)], axis=0)
    positions = jnp.arange(length)
    start = jnp.logical_or(
        jnp.any(positions[None, :, None] == bounds[:, None, :], axis=2), positions == 0
    ).astype(jnp.float32)
    keep = jnp.ones((2, length), jnp.float32)
    keeps = []
    for lag in range(1, CONV):
        keep = keep * (1.0 - jnp.pad(start, ((0, 0), (lag - 1, 0)))[:, :length])
        keeps.append(keep)
    taps = jnp.concatenate(
        [
            own_columns(conv_weight[:, :HK], hk),
            own_columns(conv_weight[:, HK : 2 * HK], hk),
            own_columns(conv_weight[:, 2 * HK :], hv),
        ],
        axis=1,
    )
    own_rate, own_bias = own_columns(log_rate, heads), own_columns(rate_bias, heads)

    rates = contract_rows(first_in, rate_in)
    rates = rates.reshape(2, length, 2 * heads)
    rate_input = rates[:, :, :heads] + own_bias
    speed = -jnp.exp(own_rate)
    decay_log = speed * jax.nn.softplus(rate_input)
    beta = jax.nn.sigmoid(rates[:, :, heads:])
    aux = jnp.concatenate([decay_log, beta] + [s[:, :, None] for s in [start] + keeps], axis=2)
    aux = jnp.pad(aux, ((0, 0), (0, 0), (0, 128 - aux.shape[2])))
    factor = jnp.concatenate([speed * jax.nn.sigmoid(rate_input), beta * (1.0 - beta)], axis=2)
    factor = jnp.pad(factor, ((0, 0), (0, 0), (0, 128 - 2 * heads)))
    mix_in, aux, factor, grad_out = lax.optimization_barrier((mix_in, aux, factor, grad_out))
    cot = plane_blocks(grad_out[0])
    conv_in = jnp.dot(first_in, mix_in, preferred_element_type=jnp.float32)
    conv_in = conv_in.astype(jnp.bfloat16).reshape(2, length, chan)
    mixed, inverses, updates, states, final = mix(conv_in, taps, aux, heads)

    mixed, gate_in, ffn = lax.optimization_barrier((mixed, gate_in, ffn))
    ffn = [along_z(w) for w in ffn]
    gate = jnp.dot(first_in, gate_in, preferred_element_type=jnp.float32).reshape(2, length, hv)
    branch = []
    for h in range(heads):
        part = mixed[:, :, h * VALUE : (h + 1) * VALUE]
        norm = lax.rsqrt(jnp.mean(part * part, axis=2, keepdims=True) + EPS)
        branch.append(
            part * norm * head_gain * jax.nn.silu(gate[:, :, h * VALUE : (h + 1) * VALUE])
        )
    branch = jnp.concatenate(branch, axis=2).astype(jnp.bfloat16).reshape(tokens, hv)
    branch, cot = lax.optimization_barrier((branch, cot))
    cot = jnp.concatenate(cot, axis=0)
    hidden = x + block_sum(row_sum([branch], [out_cols], None, F32), True, F32)

    scale_two = lax.rsqrt(jnp.mean(hidden * hidden, axis=1, keepdims=True) + EPS)
    normed_two = hidden * scale_two
    second_in = jnp.concatenate(
        plane_blocks((normed_two * ffn_norm_gain).astype(jnp.bfloat16)), axis=0
    )
    inner, d_both = [], []
    grad_ffn = jnp.zeros((width, 3 * ff), jnp.bfloat16)
    for part in range(2):
        if part:
            grad_ffn, ffn[1] = lax.optimization_barrier((grad_ffn, ffn[1]))
        weight = ffn[part]
        units = weight.shape[1] // 3
        both_in, down_in = weight[:, : 2 * units], weight[:, 2 * units :]
        both = jnp.dot(second_in, both_in, preferred_element_type=jnp.float32)
        gate_part, up_part = both[:, :units], both[:, units:]
        gate_silu = jax.nn.silu(gate_part)
        inner.append((gate_silu * up_part).astype(jnp.bfloat16))
        d_inner = jnp.dot(cot, down_in, preferred_element_type=jnp.float32)
        d_both.append(
            jnp.concatenate(
                [d_inner * up_part * silu_slope(gate_part), d_inner * gate_silu], axis=1
            ).astype(jnp.bfloat16)
        )
        for at, grad in (
            (0, contract_tokens(second_in, d_both[-1])),
            (2 * units, contract_tokens(cot, inner[-1])),
        ):
            grad_ffn = lax.dynamic_update_slice(
                grad_ffn, grad.astype(jnp.bfloat16), (0, 3 * cut * part + at)
            )
    ups = [w[:, : 2 * w.shape[1] // 3] for w in ffn]
    downs = [w[:, 2 * w.shape[1] // 3 :] for w in ffn]
    d_both = after(d_both, grad_ffn)
    grad_ffn = shard_sum(grad_ffn)
    d_second = block_sum(row_sum(d_both, ups, None, F32), False)
    grad_gain_two = jnp.sum(d_second * normed_two, axis=0)
    d_hidden = grad_out[0].astype(jnp.float32) + norm_back(
        normed_two, scale_two, d_second * ffn_norm_gain
    )

    d_mix = plane_gather(d_hidden.astype(jnp.bfloat16))
    d_branch = jnp.dot(d_mix, out_cols, preferred_element_type=jnp.float32)
    fed = product_rows(inner, downs, False).astype(jnp.bfloat16)
    d_branch, fed, final = lax.optimization_barrier((d_branch, fed, final))
    result = hidden + block_sum(row_sum(inner, downs, fed), False)
    result = result.astype(jnp.bfloat16)
    final = final.reshape(2, heads, VALUE, KEY).astype(jnp.bfloat16)
    other = swap_core(final[1])
    pair = jnp.zeros((2, heads, VALUE, KEY), jnp.bfloat16)
    pair = lax.dynamic_update_index_in_dim(pair, final[0], core, 0)
    pair = lax.dynamic_update_index_in_dim(pair, other, 1 - core, 0)
    final_state = jnp.swapaxes(laid_out(pair, "seq"), 0, 1).astype(jnp.float32)
    final_state = final_state.reshape(1, HEADS, VALUE, KEY)

    d_all, grad_taps, grad_head_gain, rate_sums = mix_back(
        conv_in,
        taps,
        aux,
        factor,
        gate,
        head_gain[None],
        mixed,
        inverses,
        updates,
        states,
        d_branch.reshape(2, length, hv),
        heads,
    )
    d_all = d_all.reshape(tokens, chan + hv + 128)
    whole_in = jnp.concatenate(
        [mix_in, gate_in, jnp.pad(rate_in.T, ((0, 0), (0, 128 - 2 * heads)))], axis=1
    )
    row_first = row_sum([d_all], [whole_in])
    grad_most = jnp.concatenate(
        [
            contract_tokens(first_in, d_all[:, 2 * hk : chan + hv]).astype(jnp.bfloat16),
            contract_tokens(d_mix, branch).astype(jnp.bfloat16),
        ],
        axis=1,
    )
    grad_most, grad_ffn, row_first = lax.optimization_barrier((grad_most, grad_ffn, row_first))
    d_first = block_sum(row_first, True)
    grad_most = shard_sum(grad_most)
    grad_last = contract_tokens(first_in, d_all[:, : 2 * hk]).astype(jnp.bfloat16)
    grad_last = to_holders(shard_sum(after(grad_last, grad_most)), split)
    grad_most = to_holders(grad_most, split)
    grad_ffn = to_holders(grad_ffn, split)
    def hidden_columns(at):
        first, second = grad_ffn[:, :, : 3 * cut], grad_ffn[:, :, 3 * cut :]
        return jnp.concatenate(
            [g[:, :, at * u : (at + 1) * u] for g, u in ((first, cut), (second, ff - cut))], axis=2
        ).reshape(rows, FF)

    grad_gate_up = jnp.concatenate([hidden_columns(0), hidden_columns(1)], axis=1)
    grad_down = hidden_columns(2)

    grad_rate = lax.dot_general(
        d_all[:, chan + hv :], first_in, (((0,), (0,)), ((), ())), preferred_element_type=jnp.float32
    )[: 2 * heads]
    small = jnp.concatenate(
        [
            grad_taps,
            grad_rate.reshape(-1, chan),
            jnp.pad(rate_sums[:2].reshape(1, -1), ((0, 0), (0, chan - 256))),
        ],
        axis=0,
    )
    small = laid_out(laid_out(axis_sum(small, "z"), "seq"), "core")
    small = small.reshape((split,) + small.shape[2:])
    grad_conv = jnp.swapaxes(small[:, :CONV], 0, 1)
    grad_conv = jnp.concatenate(
        [
            grad_conv[:, :, :hk].reshape(CONV, HK),
            grad_conv[:, :, hk : 2 * hk].reshape(CONV, HK),
            grad_conv[:, :, 2 * hk :].reshape(CONV, HV),
        ],
        axis=1,
    )
    rate_sums = small[:, -1, :256].reshape(split, 2, 128)
    grad_rate = small[:, CONV:-1].reshape(split, 2, heads, width)
    grad_rate = jnp.swapaxes(grad_rate, 0, 1).reshape(2 * HEADS, width)
    grad_rate = lax.dynamic_slice_in_dim(grad_rate, (plane * split + here) * rows, rows, 1).T

    d_first, result, final_state = lax.optimization_barrier((d_first, result, final_state))
    grad_gain_one = jnp.sum(d_first * normed, axis=0)
    sums = all_sum(jnp.concatenate([grad_gain_one, grad_gain_two, grad_head_gain[0]]))
    d_row = d_hidden + norm_back(normed, scale, d_first * norm_gain)
    d_row = d_row.astype(jnp.bfloat16)
    grad_proj = jnp.concatenate(
        [
            grad_last[:, :, :hk].reshape(rows, HK),
            grad_last[:, :, hk:].reshape(rows, HK),
            grad_most[:, :, :hv].reshape(rows, HV),
            grad_most[:, :, hv : 2 * hv].reshape(rows, HV),
        ],
        axis=1,
    )
    return (
        result[None],
        d_row[None],
        final_state,
        sums[:width],
        grad_proj,
        grad_rate,
        grad_conv,
        rate_sums[:, 0, :heads].reshape(HEADS),
        rate_sums[:, 1, :heads].reshape(HEADS),
        sums[2 * width :],
        grad_most[:, :, 2 * hv :].reshape(rows, HV),
        sums[width : 2 * width],
        grad_gate_up,
        grad_down,
    )


def solution(mesh):
    dp, seq = mesh.shape["dp"], mesh.shape["seq"]
    planes = Mesh(mesh.devices.reshape(dp // 2, 2, seq), ("z", "core", "seq"))
    row = ("z", "core")
    every = ("z", "core", "seq")
    in_specs = (
        P(row, "seq", None),
        P(row, None),
        P(),
        P(every, None),
        P(every, None),
        P(),
        P(),
        P(),
        P(),
        P(every, None),
        P(),
        P(every, None),
        P(every, None),
        P(row, "seq", None),
    )
    out_specs = (
        P(row, "seq", None),
        P(row, "seq", None),
        P(row, None, None, None),
        P(),
        P(every, None),
        P(every, None),
        P(),
        P(),
        P(),
        P(),
        P(every, None),
        P(),
        P(every, None),
        P(every, None),
    )
    return jax.shard_map(
        on_device, mesh=planes, in_specs=in_specs, out_specs=out_specs, check_vma=False
    )
```
